128 devices in a mesh: tm: 64 (over z, y, x), blk: 2 (over core).
Axes of the slice: x: 4, y: 4, z: 4, core: 2. Of those that a mesh axis runs over, the one named last changes fastest.
Arguments:
- diag_block: float32 [128, 1024, 1024], P('tm', 'blk'), may hold values from -24.5 to 25.25, as said below
- coupling: float32 [128, 1024, 1024], P('tm', 'blk'), may hold values from -12.25 to 12.25
- arrow: float32 [128, 64, 1024], P('tm', 'blk'), may hold values from -0.125 to 0.125
- corner: float32 [64, 64], P('blk'), may hold values from -6 to 6
Outputs:
- inner_pivot: float32 [64, 1024, 1024], P('tm', 'blk')
- inner_left: float32 [64, 1024, 1024], P('tm', 'blk')
- inner_right: float32 [64, 1024, 1024], P('tm', 'blk')
- inner_arrow: float32 [64, 64, 1024], P('tm', 'blk')
- pivot: float32 [64, 1024, 1024], P('tm', 'blk')
- left_factor_even: float32 [64, 1024, 1024], P('tm', 'blk')
- right_factor_even: float32 [64, 1024, 1024], P('tm', 'blk')
- arrow_factor_even: float32 [64, 64, 1024], P('tm', 'blk')
- corner_out: float32 [64, 64], P('blk')
The draws below stay inside these ranges and needn't reach their ends.
Inputs may be any that keep to these rules, and one draw needn't show every extreme that they name: `diag_block`: Symmetric; together with the coupling blocks the matrix of all day blocks is positive definite.
All inputs are finite; a program needn't handle non-finite values.
Results may differ from the reference program's by a relative error of at most 0.00014.
Values sent between devices are 32-bit elements; how exact they have to be, the bound alone decides.
A program may use at most 128 MiB of HBM per device.

```python
import jax
import jax.numpy as jnp
from jax import lax

NODES = 1024
EFFECTS = 64
DAYS = 128
N_TM = 64


def factor_rows(key, day, value_salt, scale_salt, scale_top):
    value_key = jax.random.fold_in(jax.random.fold_in(key, value_salt), day)
    scale_key = jax.random.fold_in(jax.random.fold_in(key, scale_salt), day)
    values = jax.random.randint(value_key, (NODES, NODES), -7, 8).astype(jnp.float32)
    scales = jax.random.randint(scale_key, (NODES,), 1, scale_top + 1).astype(jnp.float32)
    return values * scales[:, None]


def outer_rows(left, right):
    return lax.dot_general(left, right, (((1,), (1,)), ((), ())), precision=lax.Precision.HIGHEST, preferred_element_type=jnp.float32)


def coupling_blocks(key, scale_top, step):

    def one_day(day):
        own_rows = factor_rows(key, day, 21, 22, scale_top)
        next_rows = factor_rows(key, day, 23, 24, scale_top)
        return outer_rows(next_rows, own_rows) * step
    return lax.map(one_day, jnp.arange(DAYS, dtype=jnp.int32))


def diagonal_blocks(key, scale_top, step, shift):

    def one_day(inputs):
        day, shift_row = inputs
        own_rows = factor_rows(key, day, 21, 22, scale_top)
        earlier = jnp.maximum(day - 1, 0)
        back_rows = factor_rows(key, earlier, 23, 24, scale_top) * (day > 0).astype(jnp.float32)
        summed = outer_rows(own_rows, own_rows) + outer_rows(back_rows, back_rows)
        identity = jnp.eye(NODES, dtype=jnp.float32)
        return summed * step + shift_row[:, None] * identity
    return lax.map(one_day, (jnp.arange(DAYS, dtype=jnp.int32), shift))


def draw_coupling(key, part):
    blocks = coupling_blocks(key, 1, 2.0 ** (-14))
    return blocks


def draw_diag_block(key, part):
    shift_key = jax.random.fold_in(key, 5)
    shift = jax.random.randint(shift_key, (DAYS, NODES), 32, 97).astype(jnp.float32) * 2.0 ** (-7)
    blocks = diagonal_blocks(key, 1, 2.0 ** (-14), shift)
    return blocks


def level_of(stream_key, dims, split, least, largest):
    gain = 1.0
    for axis_at, blocks in split:
        draws = jax.random.uniform(jax.random.fold_in(jax.random.fold_in(stream_key, 6), axis_at), (blocks,), jnp.float32, least / len(split), largest / len(split))
        gain = gain * jnp.repeat(jnp.exp(draws), dims[axis_at] // blocks).reshape((-1,) + (1,) * (len(dims) - 1 - axis_at))
    return gain


def gaussian(rng, shape, spread, most, cuts=(), kind=jnp.bfloat16):
    gain = level_of(rng, shape, cuts, -0.22, 0.18) if cuts else 1.0
    result = jax.random.normal(rng, shape, jnp.float32) * spread * gain
    return jnp.minimum(jnp.maximum(result, -most), most).astype(kind)


def setup_inputs(seed: int = 0) -> dict:
    arg_keys = jax.random.split(jax.random.key(seed), 5)
    diag_block = draw_diag_block(jax.random.fold_in(arg_keys[4], 71), 0)
    coupling = draw_coupling(jax.random.fold_in(arg_keys[4], 71), 0)
    arrow = gaussian(arg_keys[2], (DAYS, EFFECTS, NODES), (DAYS * NODES // 64) ** -0.5, 0.125, ((0, 64), (1, 2)), jnp.float32)
    corner = gaussian(arg_keys[3], (EFFECTS, EFFECTS), 1.0, 6.0, ((0, 2),), jnp.float32)
    return dict(diag_block=diag_block, coupling=coupling, arrow=arrow, corner=corner)


def transposed_product(left, right):
    return lax.dot_general(left.astype(jnp.float32), right.astype(jnp.float32), (((0,), (0,)), ((), ())), precision=lax.Precision.HIGHEST, preferred_element_type=jnp.float32)

def factor_solve(pivot_rows, right_hand):
    factor = jnp.linalg.cholesky(pivot_rows)
    solved = jax.scipy.linalg.solve_triangular(factor, right_hand, lower=True)
    return (factor, solved)

def split_product(solved, node_count):
    product = transposed_product(solved, solved)
    first_first = product[:node_count, :node_count]
    second_second = product[node_count:2 * node_count, node_count:2 * node_count]
    second_first = product[node_count:2 * node_count, :node_count]
    arrow_first = product[2 * node_count:, :node_count]
    arrow_second = product[2 * node_count:, node_count:2 * node_count]
    arrow_arrow = product[2 * node_count:, 2 * node_count:]
    return (first_first, second_second, second_first, arrow_first, arrow_second, arrow_arrow)

def reference(diag_block, coupling, arrow, corner):
    partition_count = N_TM
    node_count = NODES
    open_end = (jnp.arange(partition_count) < partition_count - 1).astype(jnp.float32)

    def interior(slab_index):
        interior_day = 2 * slab_index + 1
        pivot_rows = lax.dynamic_index_in_dim(diag_block, interior_day, 0, False)
        backward = lax.dynamic_index_in_dim(coupling, 2 * slab_index, 0, False)
        forward = lax.dynamic_index_in_dim(coupling, interior_day, 0, False) * lax.dynamic_index_in_dim(open_end, slab_index, 0, False)
        arrow_part = lax.dynamic_index_in_dim(arrow, interior_day, 0, False)
        factor, solved = factor_solve(pivot_rows, jnp.concatenate([backward, forward.T, arrow_part.T], axis=1))
        blocks = split_product(solved, node_count)
        return (factor, solved[:, :node_count].T, solved[:, node_count:2 * node_count].T, solved[:, 2 * node_count:].T) + blocks
    results = lax.map(interior, jnp.arange(partition_count, dtype=jnp.int32))
    inner_pivot, inner_left, inner_right, inner_arrow = (results[0], results[1], results[2], results[3])
    first_first, second_second, second_first, arrow_first, arrow_second, arrow_arrow = results[4:]

    def shift_down(values):
        return jnp.concatenate([jnp.zeros_like(values[:1]), values[:-1]], axis=0)
    pivot = diag_block[0::2] - first_first - shift_down(second_second)
    right_coupling_block = -second_first
    arrow_factor_even = arrow[0::2] - arrow_first - shift_down(arrow_second)
    left_factor_even = shift_down(jnp.swapaxes(right_coupling_block, 1, 2))
    corner_out = corner - jnp.sum(arrow_arrow, axis=0)
    return (inner_pivot, inner_left, inner_right, inner_arrow, pivot, left_factor_even, right_coupling_block, arrow_factor_even, corner_out)
```

```python
import functools

import jax
import jax.numpy as jnp
from jax import lax
from jax.experimental import pallas as pl
from jax.experimental.pallas import tpu as pltpu
from jax.sharding import PartitionSpec as P

MESH = pl.DeviceIdType.MESH
F32 = jnp.float32
BF16 = jnp.bfloat16
NODES = 1024
HALF = 512
FX = 32
BLOCK = 128
STEPS = NODES // BLOCK
ROWS = 2 * HALF + FX
MICRO = 32
LAG = 2


def dot_nt(left, right):
    return lax.dot_general(left, right, (((1,), (1,)), ((), ())), preferred_element_type=F32)


def split(value, parts):
    out = []
    for _ in range(parts):
        piece = value.astype(BF16)
        out.append(piece)
        value = value - piece.astype(F32)
    return out


def left3(value):
    a, b, c = split(value, 3)
    return jnp.concatenate([a, a, b, a, b, c], axis=1)


def right3(value):
    a, b, c = split(value, 3)
    return jnp.concatenate([a, b, a, c, b, a], axis=1)


def left2(value):
    a, b = split(value, 2)
    return jnp.concatenate([a, b, a, b], axis=1)


def right2(value):
    a, b = split(value, 2)
    return jnp.concatenate([a, a, b, b], axis=1)


def factor_inverse(work, done):
    groups = MICRO // 8
    row_id = lax.broadcasted_iota(jnp.int32, (8, 2 * BLOCK), 0)
    twice = lambda value: jnp.concatenate([value, value], axis=1)
    for base in range(0, BLOCK, MICRO):
        rows = [work[base + 8 * g : base + 8 * g + 8, :] for g in range(groups)]
        cols = [
            [jnp.broadcast_to(rows[g][:, base + m : base + m + 1], (8, BLOCK)) for m in range(8 * g + 8)]
            for g in range(groups)
        ]
        final = [jnp.zeros((8, 2 * BLOCK), F32) for _ in range(groups)]
        for j in range(MICRO):
            gj, rj = divmod(j, 8)
            inverse = lax.rsqrt(jnp.broadcast_to(cols[gj][j][rj : rj + 1, :], (8, BLOCK)))
            pivot_row = jnp.broadcast_to(rows[gj][rj : rj + 1, :], (8, 2 * BLOCK)) * twice(inverse)
            final[gj] = jnp.where(row_id == rj, pivot_row, final[gj])
            low = [None] * groups
            for g in range(gj, groups):
                low[g] = cols[g][j] * inverse
                rows[g] = rows[g] - twice(low[g]) * pivot_row
            for m in range(j + 1, MICRO):
                gm, rm = divmod(m, 8)
                factor = jnp.broadcast_to(low[gm][rm : rm + 1, :], (8, BLOCK))
                for g in range(gm, groups):
                    cols[g][m] = cols[g][m] - low[g] * factor
        panel = jnp.concatenate(final, axis=0)
        done[base : base + MICRO, :] = panel
        rest = base + MICRO
        if rest < BLOCK:
            update = lax.dot_general(
                panel[:, :BLOCK],
                panel,
                (((0,), (0,)), ((), ())),
                precision=lax.Precision.HIGHEST,
                preferred_element_type=F32,
            )
            work[rest:, :] = work[rest:, :] - update[rest:, :]


def kernel(
    count,
    diag, coupling, arrow, corner,
    o_pivot, o_left, o_right, o_arrow, o_diag, o_lower, o_upper, o_fixed, o_corner,
    a_mat, r_mat, turn, solved, factor, arrived, sibling, forwarded,
    acc_diag, acc_lower, acc_upper, acc_fixed, acc_corner, fixed_sum,
    cat_left, cat_right, work, done,
    load_sem, out_sem, pair_send, pair_recv,
    next_send, next_recv, sib_send, sib_recv, fwd_send, fwd_recv, sum_send, sum_recv, fin_sem,
):
    p = lax.axis_index("tm")
    c = lax.axis_index("blk")
    other = 1 - c
    nxt = (lax.rem(p + 1, count), c)
    prv = (lax.rem(p + count - 1, count), c)
    sib = (p, other)
    strides = (1, 4, 16)
    spots = [lax.rem(p // s, 4) for s in strides]

    def partner(stage, d):
        spot = spots[stage]
        return (p + (lax.rem(spot + d, 4) - spot) * strides[stage], c)

    own_rows = pl.ds(pl.multiple_of(c * HALF, HALF), HALF)
    other_cols = pl.ds(pl.multiple_of(other * HALF, HALF), HALF)

    barrier = pltpu.get_barrier_semaphore()
    partners = [nxt, prv, sib] + [partner(s, d) for s in range(3) for d in (1, 2, 3)]
    for device in partners:
        pl.semaphore_signal(barrier, inc=1, device_id=device, device_id_type=MESH)

    loads = [
        pltpu.make_async_copy(diag.at[1], a_mat.at[own_rows, :], load_sem.at[0]),
        pltpu.make_async_copy(coupling.at[0, :, own_rows], turn.at[own_rows, :], load_sem.at[1]),
        pltpu.make_async_copy(coupling.at[1], r_mat.at[0:HALF, :], load_sem.at[2]),
        pltpu.make_async_copy(arrow.at[1], r_mat.at[HALF : HALF + FX, :], load_sem.at[3]),
        pltpu.make_async_copy(diag.at[0], acc_diag, load_sem.at[4]),
        pltpu.make_async_copy(arrow.at[0], acc_fixed, load_sem.at[5]),
        pltpu.make_async_copy(corner, fixed_sum, load_sem.at[6]),
    ]
    for copy in loads:
        copy.start()
    pl.semaphore_wait(barrier, len(partners))

    def remote(src, dst, send, recv, device):
        return pltpu.make_async_remote_copy(
            src_ref=src, dst_ref=dst, send_sem=send, recv_sem=recv, device_id=device, device_id_type=MESH
        )

    pairs = [
        remote(diag.at[1], a_mat.at[own_rows, :], pair_send.at[0], pair_recv.at[0], sib),
        remote(coupling.at[0, :, other_cols], turn.at[own_rows, :], pair_send.at[1], pair_recv.at[1], sib),
    ]
    for copy in pairs:
        copy.start()
    r_mat[HALF + FX :, :] = jnp.zeros((HALF, NODES), F32)
    acc_lower[...] = jnp.zeros_like(acc_lower)
    acc_upper[...] = jnp.zeros_like(acc_upper)
    acc_corner[0, spots[0]] = jnp.zeros((FX, 64), F32)
    for copy in loads:
        copy.wait()
    for copy in pairs:
        copy.wait()

    identity = (
        lax.broadcasted_iota(jnp.int32, (BLOCK, BLOCK), 0) == lax.broadcasted_iota(jnp.int32, (BLOCK, BLOCK), 1)
    ).astype(F32)
    open_end = jnp.where(p < count - 1, 1.0, 0.0).astype(F32)

    def to_next(k):
        return remote(solved.at[k], arrived.at[k], next_send.at[k], next_recv.at[k], nxt)

    def to_sibling(k):
        return remote(solved.at[k, HALF:, :], sibling.at[k], sib_send.at[k], sib_recv.at[k], sib)

    def forward(k):
        return remote(arrived.at[k, 0:HALF, :], forwarded.at[k], fwd_send.at[k], fwd_recv.at[k], sib)

    def results(k):
        cols = pl.ds(pl.multiple_of(k * BLOCK, BLOCK), BLOCK)
        return [
            pltpu.make_async_copy(factor.at[k, own_rows, :], o_pivot.at[0, :, cols], out_sem.at[0, k]),
            pltpu.make_async_copy(solved.at[k, HALF + FX :, :], o_left.at[0, :, cols], out_sem.at[1, k]),
            pltpu.make_async_copy(solved.at[k, 0:HALF, :], o_right.at[0, :, cols], out_sem.at[2, k]),
            pltpu.make_async_copy(solved.at[k, HALF : HALF + FX, :], o_arrow.at[0, :, cols], out_sem.at[3, k]),
        ]

    def chain(k):
        cols = pl.ds(pl.multiple_of(k * BLOCK, BLOCK), BLOCK)
        work[:, :BLOCK] = a_mat[cols, cols]
        work[:, BLOCK:] = identity
        factor_inverse(work, done)
        inverse = right3(done[:, BLOCK:])

        def solve_rows(i, carry):
            at = pl.ds(pl.multiple_of(i * 352, 32), 352)
            solved[k, at, :] = dot_nt(left3(r_mat[at, cols]), inverse)
            return carry

        r_mat[0:HALF, cols] = r_mat[0:HALF, cols] * open_end
        r_mat[HALF + FX :, cols] = r_mat[HALF + FX :, cols] + turn[cols, :].T
        lax.fori_loop(0, 3, solve_rows, 0)
        to_next(k).start()
        to_sibling(k).start()

        def factor_rows(i, carry):
            at = pl.ds(pl.multiple_of(i * 256, 256), 256)
            value = dot_nt(left3(a_mat[at, cols]), inverse)
            row = lax.broadcasted_iota(jnp.int32, (256, BLOCK), 0) + i * 256
            col = lax.broadcasted_iota(jnp.int32, (256, BLOCK), 1) + k * BLOCK
            value = jnp.where(row >= col, value, 0.0)
            factor[k, at, :] = value
            a, b, d = split(value, 3)
            cat_left[at, :] = jnp.concatenate([a, a, b, a, b, d], axis=1)
            cat_right[at, :] = jnp.concatenate([a, b, a, d, b, a], axis=1)
            return carry

        lax.fori_loop(0, 4, factor_rows, 0)
        for copy in results(k):
            copy.start()

    def trailing(k):
        def split_rows(i, carry):
            at = pl.ds(pl.multiple_of(i * 352, 32), 352)
            to = pl.ds(pl.multiple_of(i * 352 + NODES, 32), 352)
            cat_left[to, :] = left3(solved[k, at, :])
            return carry

        lax.fori_loop(0, 3, split_rows, 0)

        def columns(j, carry):
            cols = pl.ds(pl.multiple_of(j * 256, 256), 256)
            right = cat_right[cols, :]

            def upper(i, carry):
                at = pl.ds(pl.multiple_of(i * 256, 256), 256)
                a_mat[at, cols] = a_mat[at, cols] - dot_nt(cat_left[at, :], right)
                return carry

            lax.fori_loop(j, 4, upper, 0)

            def lower(i, carry):
                at = pl.ds(pl.multiple_of(i * 352, 32), 352)
                source = pl.ds(pl.multiple_of(i * 352 + NODES, 32), 352)
                r_mat[at, cols] = r_mat[at, cols] - dot_nt(cat_left[source, :], right)
                return carry

            lax.fori_loop(0, 3, lower, 0)
            return carry

        lax.fori_loop((k + 1) // 2, 4, columns, 0)

    def products(held, mine, theirs, first, second):
        top = left2(held[0:HALF, :])
        mid = left2(held[HALF : HALF + FX, :])
        low = left2(held[HALF + FX :, :])
        for right, cols in ((mine, own_rows), (theirs, other_cols)):
            first[:, cols] = first[:, cols] - dot_nt(top, right)
            acc_fixed[:, cols] = acc_fixed[:, cols] - dot_nt(mid, right)
            second[:, cols] = second[:, cols] - dot_nt(low, right)
        return mid

    def stage_copy(stage, d):
        slot = acc_corner.at[stage, spots[stage]]
        return remote(slot, slot, sum_send.at[stage, d - 1], sum_recv.at[stage, d - 1], partner(stage, d))

    def stage_start(stage):
        for d in (1, 2, 3):
            stage_copy(stage, d).start()

    def stage_end(stage):
        for d in (1, 2, 3):
            stage_copy(stage, d).wait()
        return acc_corner[stage, 0] + acc_corner[stage, 1] + acc_corner[stage, 2] + acc_corner[stage, 3]

    def step(k, carry):
        @pl.when(k >= LAG)
        def _():
            back = k - LAG
            to_next(back).wait()
            forward(back).start()

        @pl.when(k < STEPS)
        def _():
            chain(k)

            @pl.when(k < STEPS - 1)
            def _():
                trailing(k)

            to_sibling(k).wait()
            held = solved.at[k]
            near = sibling.at[k]
            mid = products(
                held, right2(held[HALF + FX :, :]), right2(near[FX:, :]), acc_upper, acc_diag
            )
            own = dot_nt(mid, right2(held[HALF : HALF + FX, :]))
            far = dot_nt(mid, right2(near[0:FX, :]))
            both = jnp.where(
                c == 0, jnp.concatenate([own, far], axis=1), jnp.concatenate([far, own], axis=1)
            )
            acc_corner[0, spots[0]] = acc_corner[0, spots[0]] + both

        @pl.when(k == STEPS)
        def _():
            pltpu.make_async_copy(acc_upper, o_upper.at[0], fin_sem.at[0]).start()
            stage_start(0)

        @pl.when(k >= LAG)
        def _():
            back = k - LAG
            forward(back).wait()
            held = arrived.at[back]
            products(held, right2(held[0:HALF, :]), right2(forwarded[back]), acc_diag, acc_lower)

        return carry

    lax.fori_loop(0, STEPS + LAG, step, 0)
    ends = [
        pltpu.make_async_copy(acc_diag, o_diag.at[0], fin_sem.at[1]),
        pltpu.make_async_copy(acc_lower, o_lower.at[0], fin_sem.at[2]),
        pltpu.make_async_copy(acc_fixed, o_fixed.at[0], fin_sem.at[3]),
    ]
    for copy in ends:
        copy.start()
    for stage in (1, 2):
        total = stage_end(stage - 1)
        acc_corner[stage, spots[stage]] = total
        stage_start(stage)
    fixed_sum[...] = fixed_sum[...] - stage_end(2)
    last = pltpu.make_async_copy(fixed_sum, o_corner, fin_sem.at[4])
    last.start()
    ends.append(last)
    ends.append(pltpu.make_async_copy(acc_upper, o_upper.at[0], fin_sem.at[0]))

    def drain(k, carry):
        for copy in results(k):
            copy.wait()
        return carry

    lax.fori_loop(0, STEPS, drain, 0)
    for copy in ends:
        copy.wait()


def local(count, diag_block, coupling, arrow, corner):
    block = jax.ShapeDtypeStruct((1, HALF, NODES), F32)
    strip = jax.ShapeDtypeStruct((1, FX, NODES), F32)
    any_space = pl.BlockSpec(memory_space=pl.ANY)
    dma = pltpu.SemaphoreType.DMA
    return pl.pallas_call(
        functools.partial(kernel, count),
        out_shape=(block, block, block, strip, block, block, block, strip, jax.ShapeDtypeStruct((FX, 64), F32)),
        in_specs=[any_space] * 4,
        out_specs=[any_space] * 9,
        scratch_shapes=[
            pltpu.VMEM((NODES, NODES), F32),
            pltpu.VMEM((ROWS, NODES), F32),
            pltpu.VMEM((NODES, HALF), F32),
            pltpu.VMEM((STEPS, ROWS, BLOCK), F32),
            pltpu.VMEM((STEPS, NODES, BLOCK), F32),
            pltpu.VMEM((STEPS, ROWS, BLOCK), F32),
            pltpu.VMEM((STEPS, HALF + FX, BLOCK), F32),
            pltpu.VMEM((STEPS, HALF, BLOCK), F32),
            pltpu.VMEM((HALF, NODES), F32),
            pltpu.VMEM((HALF, NODES), F32),
            pltpu.VMEM((HALF, NODES), F32),
            pltpu.VMEM((FX, NODES), F32),
            pltpu.VMEM((3, 4, FX, 64), F32),
            pltpu.VMEM((FX, 64), F32),
            pltpu.VMEM((NODES + ROWS, 6 * BLOCK), BF16),
            pltpu.VMEM((NODES, 6 * BLOCK), BF16),
            pltpu.VMEM((BLOCK, 2 * BLOCK), F32),
            pltpu.VMEM((BLOCK, 2 * BLOCK), F32),
            dma((7,)),
            dma((4, STEPS)),
            dma((2,)),
            dma((2,)),
            dma((STEPS,)),
            dma((STEPS,)),
            dma((STEPS,)),
            dma((STEPS,)),
            dma((STEPS,)),
            dma((STEPS,)),
            dma((3, 3)),
            dma((3, 3)),
            dma((5,)),
        ],
        compiler_params=pltpu.CompilerParams(
            collective_id=0, has_side_effects=True, vmem_limit_bytes=58 * 2**20
        ),
        cost_estimate=pl.CostEstimate(flops=30_000_000_000, bytes_accessed=22_000_000, transcendentals=0),
        name="eliminate",
    )(diag_block, coupling, arrow, corner)


def solution(mesh):
    rows = P("tm", "blk", None)
    placed = (rows, rows, rows, P("blk", None))
    return jax.shard_map(
        functools.partial(local, mesh.shape["tm"]),
        mesh=mesh,
        in_specs=placed,
        out_specs=(rows,) * 8 + (P("blk", None),),
        check_vma=False,
    )
```

```python
import functools

import jax
import jax.numpy as jnp
from jax import lax
from jax.experimental import pallas as pl
from jax.experimental.pallas import tpu as pltpu
from jax.sharding import PartitionSpec as P

MESH = pl.DeviceIdType.MESH
F32 = jnp.float32
BF16 = jnp.bfloat16
NODES = 1024
HALF = 512
FX = 32
BLOCK = 128
STEPS = NODES // BLOCK
ROWS = 2 * HALF + FX
MICRO = 32
WIDE = 2 * BLOCK
SUPER = NODES // WIDE
LOW = HALF + FX
CUT = ROWS - 208
RELAY = ROWS - CUT


def dot_nt(left, right):
    return lax.dot_general(left, right, (((1,), (1,)), ((), ())), preferred_element_type=F32)


def split(value, parts):
    out = []
    for _ in range(parts):
        piece = value.astype(BF16)
        out.append(piece)
        value = value - piece.astype(F32)
    return out


def left_terms(value):
    a, b, c = split(value, 3)
    return [a, a, b, a, b, c]


def right_terms(value):
    a, b, c = split(value, 3)
    return [a, b, a, c, b, a]


def joined(terms):
    return jnp.concatenate(terms, axis=1)


def left_pair(first, second):
    a, b = split(jnp.concatenate([first, second], axis=1), 2)
    return joined([a, a, b])


def right_pair(first, second):
    a, b = split(jnp.concatenate([first, second], axis=1), 2)
    return joined([a, b, a])


def factor_inverse(work, done):
    groups = MICRO // 8
    row_id = lax.broadcasted_iota(jnp.int32, (8, 2 * BLOCK), 0)
    twice = lambda value: jnp.concatenate([value, value], axis=1)
    for base in range(0, BLOCK, MICRO):
        rows = [work[base + 8 * g : base + 8 * g + 8, :] for g in range(groups)]
        cols = [
            [jnp.broadcast_to(rows[g][:, base + m : base + m + 1], (8, BLOCK)) for m in range(8 * g + 8)]
            for g in range(groups)
        ]
        final = [jnp.zeros((8, 2 * BLOCK), F32) for _ in range(groups)]
        for j in range(MICRO):
            gj, rj = divmod(j, 8)
            inverse = lax.rsqrt(jnp.broadcast_to(cols[gj][j][rj : rj + 1, :], (8, BLOCK)))
            pivot_row = jnp.broadcast_to(rows[gj][rj : rj + 1, :], (8, 2 * BLOCK)) * twice(inverse)
            final[gj] = jnp.where(row_id == rj, pivot_row, final[gj])
            low = [None] * groups
            for g in range(gj, groups):
                low[g] = cols[g][j] * inverse
                rows[g] = rows[g] - twice(low[g]) * pivot_row
            for m in range(j + 1, MICRO):
                gm, rm = divmod(m, 8)
                factor = jnp.broadcast_to(low[gm][rm : rm + 1, :], (8, BLOCK))
                for g in range(gm, groups):
                    cols[g][m] = cols[g][m] - low[g] * factor
        panel = jnp.concatenate(final, axis=0)
        done[base : base + MICRO, :] = panel
        rest = base + MICRO
        if rest < BLOCK:
            update = lax.dot_general(
                panel[:, :BLOCK],
                panel,
                (((0,), (0,)), ((), ())),
                precision=lax.Precision.HIGHEST,
                preferred_element_type=F32,
            )
            work[rest:, :] = work[rest:, :] - update[rest:, :]


def eliminate(
    count,
    diag, coupling, arrow, corner,
    solved, factor, acc_diag, acc_lower, acc_upper, acc_fixed, fixed_sum,
    a_mat, r_mat, turn, arrived, sibling, forwarded, relay_a, relay_b,
    acc_corner, cat_left, cat_right, work, done,
    a_sem, r_sem, turn_sem, load_sem, a_send, a_recv, turn_send, turn_recv,
    top_send, top_recv, low_send, low_recv, sib_send, sib_recv, fwd_send, fwd_recv,
    hop_send, hop_recv, sum_send, sum_recv,
):
    p = lax.axis_index("tm")
    c = lax.axis_index("blk")
    other = 1 - c
    strides = (1, 4, 16)
    spots = [lax.rem(p // s, 4) for s in strides]
    row_start = p - spots[0]

    def partner(stage, d):
        return (p + (lax.rem(spots[stage] + d, 4) - spots[stage]) * strides[stage], c)

    def in_row(d):
        return row_start + lax.rem(spots[0] + d, 4)

    nxt = (lax.rem(p + 1, count), c)
    prv_tm = lax.rem(p + count - 1, count)
    prv = (prv_tm, c)
    sib = (p, other)
    minus = (in_row(3), c)
    plus = (in_row(1), c)
    hop_to = (jnp.where(spots[0] == 2, lax.rem(row_start + 5, count), minus[0]), c)
    hop_from = (jnp.where(spots[0] == 1, lax.rem(row_start + count - 2, count), plus[0]), c)

    own_rows = pl.ds(pl.multiple_of(c * HALF, HALF), HALF)
    other_cols = pl.ds(pl.multiple_of(other * HALF, HALF), HALF)

    def remote(src, dst, send, recv, device):
        return pltpu.make_async_remote_copy(
            src_ref=src, dst_ref=dst, send_sem=send, recv_sem=recv, device_id=device, device_id_type=MESH
        )

    barrier = pltpu.get_barrier_semaphore()
    senders = [prv, sib, plus, hop_from] + [partner(s, d) for s in range(3) for d in (1, 2, 3)]
    for device in senders:
        pl.semaphore_signal(barrier, inc=1, device_id=device, device_id_type=MESH)

    def wide(s):
        return pl.ds(s * WIDE, WIDE)

    def half_rows(q):
        return pl.ds(pl.multiple_of(c * HALF + q * WIDE, WIDE), WIDE)

    a_loads = [
        pltpu.make_async_copy(diag.at[1, :, wide(s)], a_mat.at[own_rows, wide(s)], a_sem.at[s]) for s in range(SUPER)
    ]
    r_loads = [
        pltpu.make_async_copy(coupling.at[1, :, wide(s)], r_mat.at[0:HALF, wide(s)], r_sem.at[s])
        for s in range(SUPER)
    ]
    turn_loads = [
        pltpu.make_async_copy(coupling.at[0, wide(q), own_rows], turn.at[half_rows(q), :], turn_sem.at[q])
        for q in range(2)
    ]
    loads = [
        pltpu.make_async_copy(arrow.at[1], r_mat.at[HALF:LOW, :], load_sem.at[0]),
        pltpu.make_async_copy(diag.at[0], acc_diag.at[0], load_sem.at[1]),
        pltpu.make_async_copy(arrow.at[0], acc_fixed.at[0], load_sem.at[2]),
        pltpu.make_async_copy(corner, fixed_sum, load_sem.at[3]),
    ]
    a_pairs = [
        remote(diag.at[1, :, wide(s)], a_mat.at[own_rows, wide(s)], a_send.at[s], a_recv.at[s], sib)
        for s in range(SUPER)
    ]
    turn_pairs = [
        remote(coupling.at[0, wide(q), other_cols], turn.at[half_rows(q), :], turn_send.at[q], turn_recv.at[q], sib)
        for q in range(2)
    ]
    early = [a_loads[0], turn_loads[0], r_loads[0], loads[0]]
    late = [a_loads[1], r_loads[1], turn_loads[1], a_loads[2], r_loads[2], a_loads[3], r_loads[3]] + loads[1:]
    early_pairs = [a_pairs[0], turn_pairs[0]]
    late_pairs = [a_pairs[1], turn_pairs[1], a_pairs[2], a_pairs[3]]
    for copy in early:
        copy.start()
    pl.semaphore_wait(barrier, len(senders))
    for copy in early_pairs:
        copy.start()
    for copy in late + late_pairs:
        copy.start()
    r_mat[LOW:, :] = jnp.zeros((HALF, NODES), F32)
    acc_lower[...] = jnp.zeros_like(acc_lower)
    acc_upper[...] = jnp.zeros_like(acc_upper)
    acc_corner[0, spots[0]] = jnp.zeros((FX, 64), F32)
    identity = (
        lax.broadcasted_iota(jnp.int32, (BLOCK, BLOCK), 0) == lax.broadcasted_iota(jnp.int32, (BLOCK, BLOCK), 1)
    ).astype(F32)
    open_end = jnp.where(p < count - 1, 1.0, 0.0).astype(F32)
    for copy in early + early_pairs:
        copy.wait()

    def top_copy(k):
        return remote(solved.at[k, 0:HALF, :], arrived.at[k, 0:HALF, :], top_send.at[k], top_recv.at[k], nxt)

    def low_copy(k):
        return remote(solved.at[k, HALF:CUT, :], arrived.at[k, HALF:CUT, :], low_send.at[k], low_recv.at[k], nxt)

    def hop(stage, k):
        if stage == 0:
            return remote(solved.at[k, CUT:, :], relay_a.at[k], hop_send.at[0, k], hop_recv.at[0, k], minus)
        if stage == 1:
            return remote(relay_a.at[k], relay_b.at[k], hop_send.at[1, k], hop_recv.at[1, k], hop_to)
        return remote(relay_b.at[k], arrived.at[k, CUT:, :], hop_send.at[2, k], hop_recv.at[2, k], minus)

    def to_sibling(k):
        return remote(solved.at[k, HALF:, :], sibling.at[k], sib_send.at[k], sib_recv.at[k], sib)

    def forward(k):
        return remote(arrived.at[k, 0:HALF, :], forwarded.at[k], fwd_send.at[k], fwd_recv.at[k], sib)

    def subtract(target, rows, left, mine, theirs):
        for right, cols in ((mine, own_rows), (theirs, other_cols)):
            target[0, rows, cols] = target[0, rows, cols] - dot_nt(left, right)

    everything = slice(None)

    def local_products(s):
        e, o = 2 * s, 2 * s + 1
        mine = right_pair(solved[e, LOW:, :], solved[o, LOW:, :])
        theirs = right_pair(sibling[e, FX:, :], sibling[o, FX:, :])
        subtract(acc_upper, everything, left_pair(solved[e, 0:HALF, :], solved[o, 0:HALF, :]), mine, theirs)
        subtract(acc_diag, everything, left_pair(solved[e, LOW:, :], solved[o, LOW:, :]), mine, theirs)
        mid = left_pair(solved[e, HALF:LOW, :], solved[o, HALF:LOW, :])
        subtract(acc_fixed, everything, mid, mine, theirs)
        own = dot_nt(mid, right_pair(solved[e, HALF:LOW, :], solved[o, HALF:LOW, :]))
        far = dot_nt(mid, right_pair(sibling[e, 0:FX, :], sibling[o, 0:FX, :]))
        both = jnp.where(c == 0, joined([own, far]), joined([far, own]))
        acc_corner[0, spots[0]] = acc_corner[0, spots[0]] + both

    def arrived_sides(s):
        e, o = 2 * s, 2 * s + 1
        return (
            right_pair(arrived[e, 0:HALF, :], arrived[o, 0:HALF, :]),
            right_pair(forwarded[e], forwarded[o]),
        )

    def arrived_top(s, mine, theirs):
        e, o = 2 * s, 2 * s + 1
        subtract(acc_diag, everything, left_pair(arrived[e, 0:HALF, :], arrived[o, 0:HALF, :]), mine, theirs)

    def arrived_low(s, mine, theirs):
        e, o = 2 * s, 2 * s + 1
        subtract(acc_lower, everything, left_pair(arrived[e, LOW:, :], arrived[o, LOW:, :]), mine, theirs)
        subtract(acc_fixed, everything, left_pair(arrived[e, HALF:LOW, :], arrived[o, HALF:LOW, :]), mine, theirs)

    def half_step(s, h):
        k = 2 * s + h
        cols = pl.ds(pl.multiple_of(k * BLOCK, BLOCK), BLOCK)
        after = pl.ds(pl.multiple_of((2 * s + 1) * BLOCK, BLOCK), BLOCK)
        work[:, :BLOCK] = a_mat[cols, cols]
        work[:, BLOCK:] = identity
        factor_inverse(work, done)
        inverse = joined(right_terms(done[:, BLOCK:]))
        if h == 0:
            beside = joined(right_terms(dot_nt(joined(left_terms(a_mat[after, cols])), inverse)))

        r_mat[0:HALF, cols] = r_mat[0:HALF, cols] * open_end
        r_mat[LOW:, cols] = r_mat[LOW:, cols] + turn[cols, :].T
        value = dot_nt(joined(left_terms(r_mat[:, cols])), inverse)
        solved[k] = value
        top_copy(k).start()
        to_sibling(k).start()

        low_copy(k).start()
        hop(0, k).start()

        terms = left_terms(value)
        for t in range(6):
            cat_left[NODES:, t * WIDE + h * BLOCK : t * WIDE + (h + 1) * BLOCK] = terms[t]
        if h == 0:
            r_mat[:, after] = r_mat[:, after] - dot_nt(joined(terms), beside)

        def factor_rows(i, carry):
            at = pl.ds(pl.multiple_of(i * WIDE, WIDE), WIDE)
            value = dot_nt(joined(left_terms(a_mat[at, cols])), inverse)
            row = lax.broadcasted_iota(jnp.int32, (WIDE, BLOCK), 0) + i * WIDE
            col = lax.broadcasted_iota(jnp.int32, (WIDE, BLOCK), 1) + k * BLOCK
            value = jnp.where(row >= col, value, 0.0)

            @pl.when(i // 2 == c)
            def _():
                factor[k, pl.ds(pl.multiple_of((i - 2 * c) * WIDE, WIDE), WIDE), :] = value

            a, b, d = split(value, 3)
            for t, (x, y) in enumerate(zip([a, a, b, a, b, d], [a, b, a, d, b, a])):
                cat_left[at, t * WIDE + h * BLOCK : t * WIDE + (h + 1) * BLOCK] = x
                cat_right[at, t * WIDE + h * BLOCK : t * WIDE + (h + 1) * BLOCK] = y
            if h == 0:
                a_mat[at, after] = a_mat[at, after] - dot_nt(joined([a, a, b, a, b, d]), beside)
            return carry

        lax.fori_loop(s, SUPER, factor_rows, 0)

        def clear_rows(i, carry):
            @pl.when(i // 2 == c)
            def _():
                factor[k, pl.ds(pl.multiple_of((i - 2 * c) * WIDE, WIDE), WIDE), :] = jnp.zeros((WIDE, BLOCK), F32)

            return carry

        lax.fori_loop(0, s, clear_rows, 0)
        service(k)

    def pass_on(k):
        top_copy(k).wait()
        forward(k).start()

    def second_hop(k):
        hop(0, k).wait()
        hop(1, k).start()

    def third_hop(k):
        hop(1, k).wait()
        hop(2, k).start()

    def service(k):
        @pl.when(k >= 1)
        def _():
            second_hop(k - 1)

        @pl.when(k >= 2)
        def _():
            third_hop(k - 2)
            pass_on(k - 2)

    def trailing(s):
        def columns(j, carry):
            cols = pl.ds(pl.multiple_of(j * WIDE, WIDE), WIDE)
            right = cat_right[cols, :]

            def lower(i, carry):
                at = pl.ds(pl.multiple_of(i * WIDE, WIDE), WIDE)
                a_mat[at, cols] = a_mat[at, cols] - dot_nt(cat_left[at, :], right)
                return carry

            lax.fori_loop(j, SUPER, lower, 0)
            r_mat[:, cols] = r_mat[:, cols] - dot_nt(cat_left[NODES:, :], right)
            return carry

        lax.fori_loop(s + 1, SUPER, columns, 0)

    def super_step(s, carry):
        half_step(s, 0)
        half_step(s, 1)

        @pl.when(s == 0)
        def _():
            for copy in late + late_pairs:
                copy.wait()

        trailing(s)
        return carry

    lax.fori_loop(0, SUPER, super_step, 0)

    def stage_copy(stage, d):
        slot = acc_corner.at[stage, spots[stage]]
        return remote(slot, slot, sum_send.at[stage, d - 1], sum_recv.at[stage, d - 1], partner(stage, d))

    def stage_start(stage):
        for d in (1, 2, 3):
            stage_copy(stage, d).start()

    def stage_end(stage):
        for d in (1, 2, 3):
            stage_copy(stage, d).wait()
        return acc_corner[stage, 0] + acc_corner[stage, 1] + acc_corner[stage, 2] + acc_corner[stage, 3]

    def own(s, carry):
        to_sibling(2 * s).wait()
        to_sibling(2 * s + 1).wait()
        local_products(s)
        return carry

    def received(s, carry):
        for k in (2 * s, 2 * s + 1):
            forward(k).wait()
            low_copy(k).wait()
            hop(2, k).wait()
        mine, theirs = arrived_sides(s)
        arrived_top(s, mine, theirs)
        arrived_low(s, mine, theirs)
        return carry

    def next_stage(stage):
        total = stage_end(stage)
        acc_corner[stage + 1, spots[stage + 1]] = total
        stage_start(stage + 1)

    lax.fori_loop(0, 1, own, 0)
    second_hop(STEPS - 1)
    third_hop(STEPS - 2)
    lax.fori_loop(1, 3, own, 0)
    third_hop(STEPS - 1)
    lax.fori_loop(3, 4, own, 0)
    stage_start(0)
    lax.fori_loop(0, 2, received, 0)
    next_stage(0)
    pass_on(STEPS - 2)
    lax.fori_loop(2, 3, received, 0)
    next_stage(1)
    pass_on(STEPS - 1)
    fixed_sum[...] = fixed_sum[...] - stage_end(2)
    lax.fori_loop(3, 4, received, 0)


def store(
    solved, factor, acc_diag, acc_lower, acc_upper, acc_fixed, fixed_sum,
    o_pivot, o_left, o_right, o_arrow, o_diag, o_lower, o_upper, o_fixed, o_corner, sem,
):
    copies = [
        (acc_diag, o_diag), (acc_lower, o_lower), (acc_upper, o_upper), (acc_fixed, o_fixed), (fixed_sum, o_corner),
    ]
    for k in range(STEPS):
        cols = pl.ds(k * BLOCK, BLOCK)
        copies += [
            (factor.at[k], o_pivot.at[0, :, cols]),
            (solved.at[k, LOW:, :], o_left.at[0, :, cols]),
            (solved.at[k, 0:HALF, :], o_right.at[0, :, cols]),
            (solved.at[k, HALF:LOW, :], o_arrow.at[0, :, cols]),
        ]
    copies = [pltpu.make_async_copy(a, b, sem.at[n]) for n, (a, b) in enumerate(copies)]
    for copy in copies:
        copy.start()
    for copy in copies:
        copy.wait()


def local(count, diag_block, coupling, arrow, corner):
    def shape(*dims):
        return jax.ShapeDtypeStruct(dims, F32)

    block = shape(1, HALF, NODES)
    strip = shape(1, FX, NODES)
    fixed = shape(FX, 64)
    any_space = pl.BlockSpec(memory_space=pl.ANY)
    hbm_space = pl.BlockSpec(memory_space=pltpu.HBM)
    vmem_space = pl.BlockSpec(memory_space=pltpu.VMEM)
    dma = pltpu.SemaphoreType.DMA
    held = pl.pallas_call(
        functools.partial(eliminate, count),
        out_shape=(shape(STEPS, ROWS, BLOCK), shape(STEPS, HALF, BLOCK), block, block, block, strip, fixed),
        in_specs=[hbm_space] * 4,
        out_specs=[vmem_space] * 7,
        scratch_shapes=[
            pltpu.VMEM((NODES, NODES), F32),
            pltpu.VMEM((ROWS, NODES), F32),
            pltpu.VMEM((NODES, HALF), F32),
            pltpu.VMEM((STEPS, ROWS, BLOCK), F32),
            pltpu.VMEM((STEPS, LOW, BLOCK), F32),
            pltpu.VMEM((STEPS, HALF, BLOCK), F32),
            pltpu.VMEM((STEPS, RELAY, BLOCK), F32),
            pltpu.VMEM((STEPS, RELAY, BLOCK), F32),
            pltpu.VMEM((3, 4, FX, 64), F32),
            pltpu.VMEM((NODES + ROWS, 6 * WIDE), BF16),
            pltpu.VMEM((NODES, 6 * WIDE), BF16),
            pltpu.VMEM((BLOCK, 2 * BLOCK), F32),
            pltpu.VMEM((BLOCK, 2 * BLOCK), F32),
            dma((SUPER,)), dma((SUPER,)), dma((2,)), dma((4,)),
            dma((SUPER,)), dma((SUPER,)), dma((2,)), dma((2,)),
            dma((STEPS,)), dma((STEPS,)), dma((STEPS,)), dma((STEPS,)),
            dma((STEPS,)), dma((STEPS,)), dma((STEPS,)), dma((STEPS,)),
            dma((3, STEPS)), dma((3, STEPS)), dma((3, 3)), dma((3, 3)),
        ],
        compiler_params=pltpu.CompilerParams(
            collective_id=0, has_side_effects=True, vmem_limit_bytes=40 * 2**20
        ),
        cost_estimate=pl.CostEstimate(flops=30_000_000_000, bytes_accessed=22_000_000, transcendentals=0),
        name="eliminate",
    )(*[pltpu.with_memory_space_constraint(x, pltpu.HBM) for x in (diag_block, coupling, arrow, corner)])
    return pl.pallas_call(
        store,
        out_shape=(block, block, block, strip, block, block, block, strip, fixed),
        in_specs=[vmem_space] * 7,
        out_specs=[any_space] * 9,
        scratch_shapes=[dma((5 + 4 * STEPS,))],
        compiler_params=pltpu.CompilerParams(vmem_limit_bytes=16 * 2**20),
        name="store",
    )(*held)


def solution(mesh):
    rows = P("tm", "blk", None)
    placed = (rows, rows, rows, P("blk", None))
    return jax.shard_map(
        functools.partial(local, mesh.shape["tm"]),
        mesh=mesh,
        in_specs=placed,
        out_specs=(rows,) * 8 + (P("blk", None),),
        check_vma=False,
    )
```

```python
import functools

import jax
import jax.numpy as jnp
from jax import lax
from jax.experimental import pallas as pl
from jax.experimental.pallas import tpu as pltpu
from jax.sharding import PartitionSpec as P

MESH = pl.DeviceIdType.MESH
F32 = jnp.float32
BF16 = jnp.bfloat16
NODES = 1024
HALF = 512
FX = 32
BLOCK = 128
STEPS = NODES // BLOCK
ROWS = 2 * HALF + FX
MICRO = 32
WIDE = 2 * BLOCK
SUPER = NODES // WIDE
LOW = HALF + FX
CUT = ROWS - 256
RELAY = ROWS - CUT


def dot_nt(left, right):
    return lax.dot_general(left, right, (((1,), (1,)), ((), ())), preferred_element_type=F32)


def split(value, parts):
    out = []
    for _ in range(parts):
        piece = value.astype(BF16)
        out.append(piece)
        value = value - piece.astype(F32)
    return out


def left_terms(value, parts=3):
    if parts == 2:
        a, b = split(value, 2)
        return [a, a, b]
    a, b, c = split(value, 3)
    return [a, a, b, a, b, c]


def right_terms(value, parts=3):
    if parts == 2:
        a, b = split(value, 2)
        return [a, b, a]
    a, b, c = split(value, 3)
    return [a, b, a, c, b, a]


def joined(terms):
    return jnp.concatenate(terms, axis=1)


def left_pair(first, second):
    return joined(left_terms(joined([first, second]), 2))


def right_pair(first, second):
    return joined(right_terms(joined([first, second]), 2))


def factor_inverse(work, done, tasks=(), every=16):
    groups = MICRO // 8
    tasks = list(tasks)
    row_id = lax.broadcasted_iota(jnp.int32, (8, 2 * BLOCK), 0)
    twice = lambda value: jnp.concatenate([value, value], axis=1)
    for base in range(0, BLOCK, MICRO):
        rows = [work[base + 8 * g : base + 8 * g + 8, :] for g in range(groups)]
        cols = [
            [jnp.broadcast_to(rows[g][:, base + m : base + m + 1], (8, BLOCK)) for m in range(8 * g + 8)]
            for g in range(groups)
        ]
        final = [jnp.zeros((8, 2 * BLOCK), F32) for _ in range(groups)]
        for j in range(MICRO):
            if tasks and (base + j) % every == every - 1:
                tasks.pop(0)()
            gj, rj = divmod(j, 8)
            inverse = lax.rsqrt(jnp.broadcast_to(cols[gj][j][rj : rj + 1, :], (8, BLOCK)))
            pivot_row = jnp.broadcast_to(rows[gj][rj : rj + 1, :], (8, 2 * BLOCK)) * twice(inverse)
            final[gj] = jnp.where(row_id == rj, pivot_row, final[gj])
            low = [None] * groups
            for g in range(gj, groups):
                low[g] = cols[g][j] * inverse
                rows[g] = rows[g] - twice(low[g]) * pivot_row
            for m in range(j + 1, MICRO):
                gm, rm = divmod(m, 8)
                factor = jnp.broadcast_to(low[gm][rm : rm + 1, :], (8, BLOCK))
                for g in range(gm, groups):
                    cols[g][m] = cols[g][m] - low[g] * factor
        panel = jnp.concatenate(final, axis=0)
        done[base : base + MICRO, :] = panel
        rest = base + MICRO
        if rest < BLOCK:
            update = lax.dot_general(
                panel[:, :BLOCK],
                panel,
                (((0,), (0,)), ((), ())),
                precision=lax.Precision.HIGHEST,
                preferred_element_type=F32,
            )
            work[rest:, :] = work[rest:, :] - update[rest:, :]
    for task in tasks:
        task()


def eliminate(
    count,
    diag, coupling, arrow, corner,
    solved, factor, acc_diag, acc_lower, acc_upper, acc_fixed, fixed_sum,
    a_mat, r_mat, turn, arrived, sibling, forwarded, relay_a, relay_b,
    acc_corner, cat_left, cat_right, cat_rows, work, done,
    a_sem, r_sem, turn_sem, load_sem, a_send, a_recv, turn_send, turn_recv,
    top_send, top_recv, low_send, low_recv, sib_send, sib_recv, fwd_send, fwd_recv,
    hop_send, hop_recv, sum_send, sum_recv,
):
    p = lax.axis_index("tm")
    c = lax.axis_index("blk")
    other = 1 - c
    strides = (1, 4, 16)
    spots = [lax.rem(p // s, 4) for s in strides]
    row_start = p - spots[0]

    def partner(stage, d):
        return (p + (lax.rem(spots[stage] + d, 4) - spots[stage]) * strides[stage], c)

    def in_row(d):
        return row_start + lax.rem(spots[0] + d, 4)

    nxt = (lax.rem(p + 1, count), c)
    prv_tm = lax.rem(p + count - 1, count)
    prv = (prv_tm, c)
    sib = (p, other)
    minus = (in_row(3), c)
    plus = (in_row(1), c)
    hop_to = (jnp.where(spots[0] == 2, lax.rem(row_start + 5, count), minus[0]), c)
    hop_from = (jnp.where(spots[0] == 1, lax.rem(row_start + count - 2, count), plus[0]), c)

    own_rows = pl.ds(pl.multiple_of(c * HALF, HALF), HALF)
    other_cols = pl.ds(pl.multiple_of(other * HALF, HALF), HALF)

    def remote(src, dst, send, recv, device):
        return pltpu.make_async_remote_copy(
            src_ref=src, dst_ref=dst, send_sem=send, recv_sem=recv, device_id=device, device_id_type=MESH
        )

    barrier = pltpu.get_barrier_semaphore()
    senders = [prv, sib, plus, hop_from] + [partner(s, d) for s in range(3) for d in (1, 2, 3)]
    for device in senders:
        pl.semaphore_signal(barrier, inc=1, device_id=device, device_id_type=MESH)

    def wide(s):
        return pl.ds(s * WIDE, WIDE)

    def half_rows(q):
        return pl.ds(pl.multiple_of(c * HALF + q * WIDE, WIDE), WIDE)

    a_loads = [
        pltpu.make_async_copy(diag.at[1, :, wide(s)], a_mat.at[own_rows, wide(s)], a_sem.at[s]) for s in range(SUPER)
    ]
    r_loads = [
        pltpu.make_async_copy(coupling.at[1, :, wide(s)], r_mat.at[0:HALF, wide(s)], r_sem.at[s])
        for s in range(SUPER)
    ]
    turn_loads = [
        pltpu.make_async_copy(coupling.at[0, wide(q), own_rows], turn.at[half_rows(q), :], turn_sem.at[q])
        for q in range(2)
    ]
    loads = [
        pltpu.make_async_copy(arrow.at[1], r_mat.at[HALF:LOW, :], load_sem.at[0]),
        pltpu.make_async_copy(diag.at[0], acc_diag.at[0], load_sem.at[1]),
        pltpu.make_async_copy(arrow.at[0], acc_fixed.at[0], load_sem.at[2]),
        pltpu.make_async_copy(corner, fixed_sum, load_sem.at[3]),
    ]
    a_pairs = [
        remote(diag.at[1, :, wide(s)], a_mat.at[own_rows, wide(s)], a_send.at[s], a_recv.at[s], sib)
        for s in range(SUPER)
    ]
    turn_pairs = [
        remote(coupling.at[0, wide(q), other_cols], turn.at[half_rows(q), :], turn_send.at[q], turn_recv.at[q], sib)
        for q in range(2)
    ]
    early = [a_loads[0], turn_loads[0], r_loads[0], loads[0]]
    late = [a_loads[1], r_loads[1], turn_loads[1], a_loads[2], r_loads[2], a_loads[3], r_loads[3]] + loads[1:]
    early_pairs = [a_pairs[0], turn_pairs[0]]
    late_pairs = [a_pairs[1], turn_pairs[1], a_pairs[2], a_pairs[3]]
    for copy in early:
        copy.start()
    pl.semaphore_wait(barrier, len(senders))
    for copy in early_pairs:
        copy.start()
    for copy in late + late_pairs:
        copy.start()
    r_mat[LOW:, :] = jnp.zeros((HALF, NODES), F32)
    acc_lower[...] = jnp.zeros_like(acc_lower)
    acc_upper[...] = jnp.zeros_like(acc_upper)
    acc_corner[0, spots[0]] = jnp.zeros((FX, 64), F32)
    identity = (
        lax.broadcasted_iota(jnp.int32, (BLOCK, BLOCK), 0) == lax.broadcasted_iota(jnp.int32, (BLOCK, BLOCK), 1)
    ).astype(F32)
    open_end = jnp.where(p < count - 1, 1.0, 0.0).astype(F32)
    for copy in early + early_pairs:
        copy.wait()

    def top_copy(k):
        return remote(solved.at[k, 0:HALF, :], arrived.at[k, 0:HALF, :], top_send.at[k], top_recv.at[k], nxt)

    def low_copy(k):
        return remote(solved.at[k, HALF:CUT, :], arrived.at[k, HALF:CUT, :], low_send.at[k], low_recv.at[k], nxt)

    def hop(stage, k):
        if stage == 0:
            return remote(solved.at[k, CUT:, :], relay_a.at[k], hop_send.at[0, k], hop_recv.at[0, k], minus)
        if stage == 1:
            return remote(relay_a.at[k], relay_b.at[k], hop_send.at[1, k], hop_recv.at[1, k], hop_to)
        return remote(relay_b.at[k], arrived.at[k, CUT:, :], hop_send.at[2, k], hop_recv.at[2, k], minus)

    def to_sibling(k):
        return remote(solved.at[k, HALF:, :], sibling.at[k], sib_send.at[k], sib_recv.at[k], sib)

    def forward(k):
        return remote(arrived.at[k, 0:HALF, :], forwarded.at[k], fwd_send.at[k], fwd_recv.at[k], sib)

    def tile(base, q):
        return pl.ds(pl.multiple_of(base * HALF + q * WIDE, WIDE), WIDE)

    def product_tasks(top, low, mine, theirs, first, second):
        tasks = []
        for right, base in ((mine, c), (theirs, other)):
            for q in range(2):
                piece = right[q * WIDE : (q + 1) * WIDE, :]
                cols = tile(base, q)

                def upper(piece=piece, cols=cols):
                    first[0, :, cols] = first[0, :, cols] - dot_nt(top, piece)

                def lower(piece=piece, cols=cols):
                    value = dot_nt(low, piece)
                    acc_fixed[0, :, cols] = acc_fixed[0, :, cols] - value[0:FX, :]
                    second[0, :, cols] = second[0, :, cols] - value[FX:, :]

                tasks += [upper, lower]
        return tasks

    def local_tasks(s):
        e, o = 2 * s, 2 * s + 1
        low = cat_rows[HALF:, :]
        far = right_pair(sibling[e], sibling[o])
        near = joined([low[:, 0:WIDE], low[:, 2 * WIDE :], low[:, 0:WIDE]])

        def fixed():
            mid = low[0:FX, :]
            own, their = dot_nt(mid, near[0:FX, :]), dot_nt(mid, far[0:FX, :])
            both = jnp.where(c == 0, joined([own, their]), joined([their, own]))
            acc_corner[0, spots[0]] = acc_corner[0, spots[0]] + both

        return product_tasks(cat_rows[0:HALF, :], low, near[FX:, :], far[FX:, :], acc_upper, acc_diag) + [fixed]

    def received_tasks(s):
        e, o = 2 * s, 2 * s + 1
        return product_tasks(
            left_pair(arrived[e, 0:HALF, :], arrived[o, 0:HALF, :]),
            left_pair(arrived[e, HALF:, :], arrived[o, HALF:, :]),
            right_pair(arrived[e, 0:HALF, :], arrived[o, 0:HALF, :]),
            right_pair(forwarded[e], forwarded[o]),
            acc_diag,
            acc_lower,
        )

    def received_block_tasks(k):
        return product_tasks(
            joined(left_terms(arrived[k, 0:HALF, :], 2)),
            joined(left_terms(arrived[k, HALF:, :], 2)),
            joined(right_terms(arrived[k, 0:HALF, :], 2)),
            joined(right_terms(forwarded[k], 2)),
            acc_diag,
            acc_lower,
        )

    def await_received(k):
        forward(k).wait()
        low_copy(k).wait()
        hop(2, k).wait()

    def half_step(s, h):
        k = 2 * s + h
        cols = pl.ds(pl.multiple_of(k * BLOCK, BLOCK), BLOCK)
        after = pl.ds(pl.multiple_of((2 * s + 1) * BLOCK, BLOCK), BLOCK)
        work[:, :BLOCK] = a_mat[cols, cols]
        work[:, BLOCK:] = identity
        if h == 0:

            @pl.when(s == 0)
            def _():
                factor_inverse(work, done)

            @pl.when(s >= 1)
            def _():
                to_sibling(2 * s - 2).wait()
                to_sibling(2 * s - 1).wait()
                factor_inverse(work, done, local_tasks(s - 1))
        else:

            @pl.when(s < 2)
            def _():
                factor_inverse(work, done)

            @pl.when(s >= 2)
            def _():
                await_received(2 * s - 4)
                await_received(2 * s - 3)
                factor_inverse(work, done, received_tasks(s - 2))

        inverse = joined(right_terms(done[:, BLOCK:]))
        if h == 0:
            beside = joined(right_terms(dot_nt(joined(left_terms(a_mat[after, cols])), inverse)))

        r_mat[0:HALF, cols] = r_mat[0:HALF, cols] * open_end
        r_mat[LOW:, cols] = r_mat[LOW:, cols] + turn[cols, :].T
        value = dot_nt(joined(left_terms(r_mat[:, cols], 2)), inverse[:, : 3 * BLOCK])
        solved[k] = value
        top_copy(k).start()
        to_sibling(k).start()

        low_copy(k).start()
        hop(0, k).start()

        terms = left_terms(value, 2)
        for t in range(3):
            cat_rows[:, t * WIDE + h * BLOCK : t * WIDE + (h + 1) * BLOCK] = terms[t]
        if h == 0:
            r_mat[:, after] = r_mat[:, after] - dot_nt(joined(terms), beside[:, : 3 * BLOCK])

        def factor_rows(i, carry):
            at = pl.ds(pl.multiple_of(i * WIDE, WIDE), WIDE)
            value = dot_nt(joined(left_terms(a_mat[at, cols])), inverse)
            row = lax.broadcasted_iota(jnp.int32, (WIDE, BLOCK), 0) + i * WIDE
            col = lax.broadcasted_iota(jnp.int32, (WIDE, BLOCK), 1) + k * BLOCK
            value = jnp.where(row >= col, value, 0.0)

            @pl.when(i // 2 == c)
            def _():
                factor[k, pl.ds(pl.multiple_of((i - 2 * c) * WIDE, WIDE), WIDE), :] = value

            a, b, d = split(value, 3)
            for t, (x, y) in enumerate(zip([a, a, b, a, b, d], [a, b, a, d, b, a])):
                cat_left[at, t * WIDE + h * BLOCK : t * WIDE + (h + 1) * BLOCK] = x
                cat_right[at, t * WIDE + h * BLOCK : t * WIDE + (h + 1) * BLOCK] = y
            if h == 0:
                a_mat[at, after] = a_mat[at, after] - dot_nt(joined([a, a, b, a, b, d]), beside)
            return carry

        lax.fori_loop(s, SUPER, factor_rows, 0)

        def clear_rows(i, carry):
            @pl.when(i // 2 == c)
            def _():
                factor[k, pl.ds(pl.multiple_of((i - 2 * c) * WIDE, WIDE), WIDE), :] = jnp.zeros((WIDE, BLOCK), F32)

            return carry

        lax.fori_loop(0, s, clear_rows, 0)
        service(k)

    def pass_on(k):
        top_copy(k).wait()
        forward(k).start()

    def second_hop(k):
        hop(0, k).wait()
        hop(1, k).start()

    def third_hop(k):
        hop(1, k).wait()
        hop(2, k).start()

    def service(k):
        @pl.when(k >= 1)
        def _():
            second_hop(k - 1)

        @pl.when(k >= 2)
        def _():
            third_hop(k - 2)
            pass_on(k - 2)

    def trailing(s):
        def columns(j, carry):
            cols = pl.ds(pl.multiple_of(j * WIDE, WIDE), WIDE)
            right = cat_right[cols, :]

            def lower(i, carry):
                at = pl.ds(pl.multiple_of(i * WIDE, WIDE), WIDE)
                a_mat[at, cols] = a_mat[at, cols] - dot_nt(cat_left[at, :], right)
                return carry

            lax.fori_loop(j, SUPER, lower, 0)
            r_mat[:, cols] = r_mat[:, cols] - dot_nt(cat_rows[...], right[:, : 3 * WIDE])
            return carry

        lax.fori_loop(s + 1, SUPER, columns, 0)

    def super_step(s, carry):
        half_step(s, 0)
        half_step(s, 1)

        @pl.when(s == 0)
        def _():
            for copy in late + late_pairs:
                copy.wait()

        trailing(s)
        return carry

    lax.fori_loop(0, SUPER, super_step, 0)

    def stage_copy(stage, d):
        slot = acc_corner.at[stage, spots[stage]]
        return remote(slot, slot, sum_send.at[stage, d - 1], sum_recv.at[stage, d - 1], partner(stage, d))

    def stage_start(stage):
        for d in (1, 2, 3):
            stage_copy(stage, d).start()

    def stage_end(stage):
        for d in (1, 2, 3):
            stage_copy(stage, d).wait()
        return acc_corner[stage, 0] + acc_corner[stage, 1] + acc_corner[stage, 2] + acc_corner[stage, 3]

    def next_stage(stage):
        total = stage_end(stage)
        acc_corner[stage + 1, spots[stage + 1]] = total
        stage_start(stage + 1)

    second_hop(STEPS - 1)
    third_hop(STEPS - 2)
    to_sibling(STEPS - 2).wait()
    to_sibling(STEPS - 1).wait()
    for task in local_tasks(SUPER - 1):
        task()
    stage_start(0)
    third_hop(STEPS - 1)
    await_received(STEPS - 4)
    await_received(STEPS - 3)
    for task in received_tasks(SUPER - 2):
        task()
    next_stage(0)
    pass_on(STEPS - 2)
    await_received(STEPS - 2)
    for task in received_block_tasks(STEPS - 2):
        task()
    next_stage(1)
    pass_on(STEPS - 1)
    fixed_sum[...] = fixed_sum[...] - stage_end(2)
    await_received(STEPS - 1)
    for task in received_block_tasks(STEPS - 1):
        task()


def store(
    solved, factor, acc_diag, acc_lower, acc_upper, acc_fixed, fixed_sum,
    o_pivot, o_left, o_right, o_arrow, o_diag, o_lower, o_upper, o_fixed, o_corner, sem,
):
    copies = [
        (acc_diag, o_diag), (acc_lower, o_lower), (acc_upper, o_upper), (acc_fixed, o_fixed), (fixed_sum, o_corner),
    ]
    for k in range(STEPS):
        cols = pl.ds(k * BLOCK, BLOCK)
        copies += [
            (factor.at[k], o_pivot.at[0, :, cols]),
            (solved.at[k, LOW:, :], o_left.at[0, :, cols]),
            (solved.at[k, 0:HALF, :], o_right.at[0, :, cols]),
            (solved.at[k, HALF:LOW, :], o_arrow.at[0, :, cols]),
        ]
    copies = [pltpu.make_async_copy(a, b, sem.at[n]) for n, (a, b) in enumerate(copies)]
    for copy in copies:
        copy.start()
    for copy in copies:
        copy.wait()


def local(count, diag_block, coupling, arrow, corner):
    def shape(*dims):
        return jax.ShapeDtypeStruct(dims, F32)

    block = shape(1, HALF, NODES)
    strip = shape(1, FX, NODES)
    fixed = shape(FX, 64)
    any_space = pl.BlockSpec(memory_space=pl.ANY)
    hbm_space = pl.BlockSpec(memory_space=pltpu.HBM)
    vmem_space = pl.BlockSpec(memory_space=pltpu.VMEM)
    dma = pltpu.SemaphoreType.DMA
    held = pl.pallas_call(
        functools.partial(eliminate, count),
        out_shape=(shape(STEPS, ROWS, BLOCK), shape(STEPS, HALF, BLOCK), block, block, block, strip, fixed),
        in_specs=[hbm_space] * 4,
        out_specs=[vmem_space] * 7,
        scratch_shapes=[
            pltpu.VMEM((NODES, NODES), F32),
            pltpu.VMEM((ROWS, NODES), F32),
            pltpu.VMEM((NODES, HALF), F32),
            pltpu.VMEM((STEPS, ROWS, BLOCK), F32),
            pltpu.VMEM((STEPS, LOW, BLOCK), F32),
            pltpu.VMEM((STEPS, HALF, BLOCK), F32),
            pltpu.VMEM((STEPS, RELAY, BLOCK), F32),
            pltpu.VMEM((STEPS, RELAY, BLOCK), F32),
            pltpu.VMEM((3, 4, FX, 64), F32),
            pltpu.VMEM((NODES, 6 * WIDE), BF16),
            pltpu.VMEM((NODES, 6 * WIDE), BF16),
            pltpu.VMEM((ROWS, 3 * WIDE), BF16),
            pltpu.VMEM((BLOCK, 2 * BLOCK), F32),
            pltpu.VMEM((BLOCK, 2 * BLOCK), F32),
            dma((SUPER,)), dma((SUPER,)), dma((2,)), dma((4,)),
            dma((SUPER,)), dma((SUPER,)), dma((2,)), dma((2,)),
            dma((STEPS,)), dma((STEPS,)), dma((STEPS,)), dma((STEPS,)),
            dma((STEPS,)), dma((STEPS,)), dma((STEPS,)), dma((STEPS,)),
            dma((3, STEPS)), dma((3, STEPS)), dma((3, 3)), dma((3, 3)),
        ],
        compiler_params=pltpu.CompilerParams(
            collective_id=0, has_side_effects=True, vmem_limit_bytes=40 * 2**20
        ),
        cost_estimate=pl.CostEstimate(flops=30_000_000_000, bytes_accessed=22_000_000, transcendentals=0),
        name="eliminate",
    )(*[pltpu.with_memory_space_constraint(x, pltpu.HBM) for x in (diag_block, coupling, arrow, corner)])
    return pl.pallas_call(
        store,
        out_shape=(block, block, block, strip, block, block, block, strip, fixed),
        in_specs=[vmem_space] * 7,
        out_specs=[any_space] * 9,
        scratch_shapes=[dma((5 + 4 * STEPS,))],
        compiler_params=pltpu.CompilerParams(vmem_limit_bytes=16 * 2**20),
        name="store",
    )(*held)


def solution(mesh):
    rows = P("tm", "blk", None)
    placed = (rows, rows, rows, P("blk", None))
    return jax.shard_map(
        functools.partial(local, mesh.shape["tm"]),
        mesh=mesh,
        in_specs=placed,
        out_specs=(rows,) * 8 + (P("blk", None),),
        check_vma=False,
    )
```

```python
import functools

import jax
import jax.numpy as jnp
from jax import lax
from jax.experimental import pallas as pl
from jax.experimental.pallas import tpu as pltpu
from jax.sharding import PartitionSpec as P

MESH = pl.DeviceIdType.MESH
F32 = jnp.float32
BF16 = jnp.bfloat16
NODES = 1024
HALF = 512
FX = 32
BLOCK = 128
STEPS = NODES // BLOCK
ROWS = 2 * HALF + FX
MICRO = 32
IN_FLIGHT = 2
WIDE = 2 * BLOCK
SUPER = NODES // WIDE
LOW = HALF + FX
CUT = ROWS - 240
RELAY = ROWS - CUT


def dot_nt(left, right):
    return lax.dot_general(left, right, (((1,), (1,)), ((), ())), preferred_element_type=F32)


def split(value, parts):
    out = []
    for _ in range(parts):
        piece = value.astype(BF16)
        out.append(piece)
        value = value - piece.astype(F32)
    return out


def left_terms(value, parts=3):
    if parts == 2:
        a, b = split(value, 2)
        return [a, a, b]
    a, b, c = split(value, 3)
    return [a, a, b, a, b, c]


def right_terms(value, parts=3):
    if parts == 2:
        a, b = split(value, 2)
        return [a, b, a]
    a, b, c = split(value, 3)
    return [a, b, a, c, b, a]


def joined(terms):
    return jnp.concatenate(terms, axis=1)


def left_pair(first, second):
    return joined(left_terms(joined([first, second]), 2))


def right_pair(first, second):
    return joined(right_terms(joined([first, second]), 2))


def factor_inverse(work, done, tasks=(), every=16):
    groups = MICRO // 8
    tasks = list(tasks)
    row_id = lax.broadcasted_iota(jnp.int32, (8, 2 * BLOCK), 0)
    twice = lambda value: jnp.concatenate([value, value], axis=1)
    for base in range(0, BLOCK, MICRO):
        rows = [work[base + 8 * g : base + 8 * g + 8, :] for g in range(groups)]
        cols = [
            [jnp.broadcast_to(rows[g][:, base + m : base + m + 1], (8, BLOCK)) for m in range(8 * g + 8)]
            for g in range(groups)
        ]
        final = [jnp.zeros((8, 2 * BLOCK), F32) for _ in range(groups)]
        for j in range(MICRO):
            if tasks and (base + j) % every == every - 1:
                tasks.pop(0)()
            gj, rj = divmod(j, 8)
            inverse = lax.rsqrt(jnp.broadcast_to(cols[gj][j][rj : rj + 1, :], (8, BLOCK)))
            pivot_row = jnp.broadcast_to(rows[gj][rj : rj + 1, :], (8, 2 * BLOCK)) * twice(inverse)
            final[gj] = jnp.where(row_id == rj, pivot_row, final[gj])
            low = [None] * groups
            for g in range(gj, groups):
                low[g] = cols[g][j] * inverse
                rows[g] = rows[g] - twice(low[g]) * pivot_row
            for m in range(j + 1, MICRO):
                gm, rm = divmod(m, 8)
                factor = jnp.broadcast_to(low[gm][rm : rm + 1, :], (8, BLOCK))
                for g in range(gm, groups):
                    cols[g][m] = cols[g][m] - low[g] * factor
        panel = jnp.concatenate(final, axis=0)
        done[base : base + MICRO, :] = panel
        rest = base + MICRO
        if rest < BLOCK:
            update = lax.dot_general(
                panel[:, :BLOCK],
                panel,
                (((0,), (0,)), ((), ())),
                precision=lax.Precision.HIGHEST,
                preferred_element_type=F32,
            )
            work[rest:, :] = work[rest:, :] - update[rest:, :]
    for task in tasks:
        task()


def eliminate(
    count,
    diag, coupling, arrow, corner,
    solved, factor, acc_diag, acc_lower, acc_upper, acc_fixed, fixed_sum,
    a_mat, r_mat, turn, arrived, sibling, forwarded, relay_a, relay_b,
    acc_corner, cat_left, cat_right, cat_rows, work, done, lead, lead_in,
    a_sem, r_sem, turn_sem, load_sem, a_send, a_recv, turn_send, turn_recv,
    top_send, top_recv, low_send, low_recv, sib_send, sib_recv, fwd_send, fwd_recv,
    hop_send, hop_recv, sum_send, sum_recv, lead_send, lead_recv,
):
    p = lax.axis_index("tm")
    c = lax.axis_index("blk")
    other = 1 - c
    strides = (16, 4, 1)
    spots = [lax.rem(p // s, 4) for s in strides]
    spot = spots[2]
    row_start = p - spot

    def partner(stage, d):
        return (p + (lax.rem(spots[stage] + d, 4) - spots[stage]) * strides[stage], c)

    def in_row(d):
        return row_start + lax.rem(spot + d, 4)

    nxt = (lax.rem(p + 1, count), c)
    prv_tm = lax.rem(p + count - 1, count)
    prv = (prv_tm, c)
    sib = (p, other)
    minus = (in_row(3), c)
    plus = (in_row(1), c)
    hop_to = (jnp.where(spot == 2, lax.rem(row_start + 5, count), minus[0]), c)
    hop_from = (jnp.where(spot == 1, lax.rem(row_start + count - 2, count), plus[0]), c)

    own_rows = pl.ds(pl.multiple_of(c * HALF, HALF), HALF)
    other_cols = pl.ds(pl.multiple_of(other * HALF, HALF), HALF)

    def remote(src, dst, send, recv, device):
        return pltpu.make_async_remote_copy(
            src_ref=src, dst_ref=dst, send_sem=send, recv_sem=recv, device_id=device, device_id_type=MESH
        )

    barrier = pltpu.get_barrier_semaphore()
    senders = [prv, sib, plus, hop_from] + [partner(s, d) for s in range(3) for d in (1, 2, 3)]
    for device in senders:
        pl.semaphore_signal(barrier, inc=1, device_id=device, device_id_type=MESH)

    def wide(s):
        return pl.ds(s * WIDE, WIDE)

    def half_rows(q):
        return pl.ds(pl.multiple_of(c * HALF + q * WIDE, WIDE), WIDE)

    a_loads = [
        pltpu.make_async_copy(diag.at[1, :, wide(s)], a_mat.at[own_rows, wide(s)], a_sem.at[s]) for s in range(SUPER)
    ]
    r_loads = [
        pltpu.make_async_copy(coupling.at[1, :, wide(s)], r_mat.at[0:HALF, wide(s)], r_sem.at[s])
        for s in range(SUPER)
    ]
    turn_loads = [
        pltpu.make_async_copy(coupling.at[0, wide(q), own_rows], turn.at[half_rows(q), :], turn_sem.at[q])
        for q in range(2)
    ]
    loads = [
        pltpu.make_async_copy(arrow.at[1], r_mat.at[HALF:LOW, :], load_sem.at[0]),
        pltpu.make_async_copy(diag.at[0], acc_diag.at[0], load_sem.at[1]),
        pltpu.make_async_copy(arrow.at[0], acc_fixed.at[0], load_sem.at[2]),
        pltpu.make_async_copy(corner, fixed_sum, load_sem.at[3]),
    ]
    a_pairs = [
        remote(diag.at[1, :, wide(s)], a_mat.at[own_rows, wide(s)], a_send.at[s], a_recv.at[s], sib)
        for s in range(SUPER)
    ]
    turn_pairs = [
        remote(coupling.at[0, wide(q), other_cols], turn.at[half_rows(q), :], turn_send.at[q], turn_recv.at[q], sib)
        for q in range(2)
    ]
    early = [a_loads[0], turn_loads[0], r_loads[0], loads[0]]
    late = [a_loads[1], r_loads[1], turn_loads[1], a_loads[2], r_loads[2], a_loads[3], r_loads[3]] + loads[1:]
    early_pairs = [a_pairs[0], turn_pairs[0]]
    late_pairs = [a_pairs[1], turn_pairs[1], a_pairs[2], a_pairs[3]]
    for copy in early:
        copy.start()
    pl.semaphore_wait(barrier, len(senders))
    for copy in early_pairs:
        copy.start()
    raw_top = remote(
        coupling.at[1, :, pl.ds(0, BLOCK)], arrived.at[0, 0:HALF, :], top_send.at[0], top_recv.at[0], nxt
    )
    raw_top.start()
    lead_copy = remote(lead, lead_in, lead_send, lead_recv, nxt)
    for copy in late + late_pairs:
        copy.start()
    r_mat[LOW:, :] = jnp.zeros((HALF, NODES), F32)
    acc_lower[...] = jnp.zeros_like(acc_lower)
    acc_upper[...] = jnp.zeros_like(acc_upper)
    acc_corner[0, spots[0]] = jnp.zeros((FX, 64), F32)
    identity = (
        lax.broadcasted_iota(jnp.int32, (BLOCK, BLOCK), 0) == lax.broadcasted_iota(jnp.int32, (BLOCK, BLOCK), 1)
    ).astype(F32)
    open_end = jnp.where(p < count - 1, 1.0, 0.0).astype(F32)
    open_start = jnp.where(p > 0, 1.0, 0.0).astype(F32)
    for copy in early + early_pairs:
        copy.wait()

    def top_copy(k):
        return remote(solved.at[k, 0:HALF, :], arrived.at[k, 0:HALF, :], top_send.at[k], top_recv.at[k], nxt)

    def low_copy(k):
        return remote(solved.at[k, HALF:CUT, :], arrived.at[k, HALF:CUT, :], low_send.at[k], low_recv.at[k], nxt)

    def hop(stage, k):
        if stage == 0:
            return remote(solved.at[k, CUT:, :], relay_a.at[k], hop_send.at[0, k], hop_recv.at[0, k], minus)
        if stage == 1:
            return remote(relay_a.at[k], relay_b.at[k], hop_send.at[1, k], hop_recv.at[1, k], hop_to)
        return remote(relay_b.at[k], arrived.at[k, CUT:, :], hop_send.at[2, k], hop_recv.at[2, k], minus)

    def to_sibling(k):
        return remote(solved.at[k, HALF:, :], sibling.at[k], sib_send.at[k], sib_recv.at[k], sib)

    def forward(k):
        return remote(arrived.at[k, 0:HALF, :], forwarded.at[k], fwd_send.at[k], fwd_recv.at[k], sib)

    def tile(base, q):
        return pl.ds(pl.multiple_of(base * HALF + q * WIDE, WIDE), WIDE)

    def product_tasks(top, low, mine, theirs, first, second):
        tasks = []
        for right, base in ((mine, c), (theirs, other)):
            for q in range(2):
                piece = right[q * WIDE : (q + 1) * WIDE, :]
                cols = tile(base, q)

                def upper(piece=piece, cols=cols):
                    first[0, :, cols] = first[0, :, cols] - dot_nt(top, piece)

                def lower(piece=piece, cols=cols):
                    value = dot_nt(low, piece)
                    acc_fixed[0, :, cols] = acc_fixed[0, :, cols] - value[0:FX, :]
                    second[0, :, cols] = second[0, :, cols] - value[FX:, :]

                tasks += [upper, lower]
        return tasks

    def local_tasks(s):
        e, o = 2 * s, 2 * s + 1
        low = cat_rows[HALF:, :]
        far = right_pair(sibling[e], sibling[o])
        near = joined([low[:, 0:WIDE], low[:, 2 * WIDE :], low[:, 0:WIDE]])

        def fixed():
            mid = low[0:FX, :]
            own, their = dot_nt(mid, near[0:FX, :]), dot_nt(mid, far[0:FX, :])
            both = jnp.where(c == 0, joined([own, their]), joined([their, own]))
            acc_corner[0, spots[0]] = acc_corner[0, spots[0]] + both

        return product_tasks(cat_rows[0:HALF, :], low, near[FX:, :], far[FX:, :], acc_upper, acc_diag) + [fixed]

    def received_tasks(s):
        e, o = 2 * s, 2 * s + 1
        return product_tasks(
            left_pair(arrived[e, 0:HALF, :], arrived[o, 0:HALF, :]),
            left_pair(arrived[e, HALF:, :], arrived[o, HALF:, :]),
            right_pair(arrived[e, 0:HALF, :], arrived[o, 0:HALF, :]),
            right_pair(forwarded[e], forwarded[o]),
            acc_diag,
            acc_lower,
        )

    def received_block_tasks(k):
        return product_tasks(
            joined(left_terms(arrived[k, 0:HALF, :], 2)),
            joined(left_terms(arrived[k, HALF:, :], 2)),
            joined(right_terms(arrived[k, 0:HALF, :], 2)),
            joined(right_terms(forwarded[k], 2)),
            acc_diag,
            acc_lower,
        )

    def await_received(k):
        forward(k).wait()
        low_copy(k).wait_recv()
        hop(2, k).wait()

    def half_step(s, h):
        k = 2 * s + h
        cols = pl.ds(pl.multiple_of(k * BLOCK, BLOCK), BLOCK)
        after = pl.ds(pl.multiple_of((2 * s + 1) * BLOCK, BLOCK), BLOCK)
        work[:, :BLOCK] = a_mat[cols, cols]
        work[:, BLOCK:] = identity
        if h == 0:

            @pl.when(s == 0)
            def _():
                factor_inverse(work, done)

            @pl.when(s >= 1)
            def _():
                to_sibling(2 * s - 2).wait()
                to_sibling(2 * s - 1).wait()
                factor_inverse(work, done, local_tasks(s - 1))
        else:

            @pl.when(s < 2)
            def _():
                factor_inverse(work, done)

            @pl.when(s >= 2)
            def _():
                await_received(2 * s - 4)
                await_received(2 * s - 3)
                factor_inverse(work, done, received_tasks(s - 2))

        inverse = joined(right_terms(done[:, BLOCK:]))
        if h == 0:
            beside = joined(right_terms(dot_nt(joined(left_terms(a_mat[after, cols])), inverse)))

        r_mat[0:HALF, cols] = r_mat[0:HALF, cols] * open_end
        r_mat[LOW:, cols] = r_mat[LOW:, cols] + turn[cols, :].T
        value = dot_nt(joined(left_terms(r_mat[:, cols], 2)), inverse[:, : 3 * BLOCK])
        solved[k] = value
        @pl.when(k >= IN_FLIGHT)
        def _():
            sent(k - IN_FLIGHT)

        if h == 0:

            @pl.when(s == 0)
            def _():
                lead[...] = done[:, BLOCK:]
                lead_copy.start()

            @pl.when(s > 0)
            def _():
                top_copy(k).start()
        else:
            top_copy(k).start()
        to_sibling(k).start()

        low_copy(k).start()
        hop(0, k).start()

        terms = left_terms(value, 2)
        for t in range(3):
            cat_rows[:, t * WIDE + h * BLOCK : t * WIDE + (h + 1) * BLOCK] = terms[t]
        if h == 0:
            r_mat[:, after] = r_mat[:, after] - dot_nt(joined(terms), beside[:, : 3 * BLOCK])

        def factor_rows(i, carry):
            at = pl.ds(pl.multiple_of(i * WIDE, WIDE), WIDE)
            value = dot_nt(joined(left_terms(a_mat[at, cols])), inverse)
            row = lax.broadcasted_iota(jnp.int32, (WIDE, BLOCK), 0) + i * WIDE
            col = lax.broadcasted_iota(jnp.int32, (WIDE, BLOCK), 1) + k * BLOCK
            value = jnp.where(row >= col, value, 0.0)

            @pl.when(i // 2 == c)
            def _():
                factor[k, pl.ds(pl.multiple_of((i - 2 * c) * WIDE, WIDE), WIDE), :] = value

            a, b, d = split(value, 3)
            for t, (x, y) in enumerate(zip([a, a, b, a, b, d], [a, b, a, d, b, a])):
                cat_left[at, t * WIDE + h * BLOCK : t * WIDE + (h + 1) * BLOCK] = x
                cat_right[at, t * WIDE + h * BLOCK : t * WIDE + (h + 1) * BLOCK] = y
            if h == 0:
                a_mat[at, after] = a_mat[at, after] - dot_nt(joined([a, a, b, a, b, d]), beside)
            return carry

        lax.fori_loop(s, SUPER, factor_rows, 0)

        def clear_rows(i, carry):
            @pl.when(i // 2 == c)
            def _():
                factor[k, pl.ds(pl.multiple_of((i - 2 * c) * WIDE, WIDE), WIDE), :] = jnp.zeros((WIDE, BLOCK), F32)

            return carry

        lax.fori_loop(0, s, clear_rows, 0)
        if h == 0:
            service(k)
        else:

            @pl.when(s < SUPER - 1)
            def _():
                service(k)


    def sent(k):
        top_copy(k).wait_send()
        low_copy(k).wait_send()

    def pass_on(k):
        top_copy(k).wait_recv()
        forward(k).start()

    def second_hop(k):
        hop(0, k).wait()
        hop(1, k).start()

    def third_hop(k):
        hop(1, k).wait()
        hop(2, k).start()

    def service(k):
        @pl.when(k >= 1)
        def _():
            second_hop(k - 1)

        @pl.when(k >= 2)
        def _():
            third_hop(k - 2)

        @pl.when(k == 2)
        def _():
            raw_top.wait_recv()
            lead_copy.wait()
            raw = arrived[0, 0:HALF, :] * open_start
            arrived[0, 0:HALF, :] = dot_nt(
                joined(left_terms(raw, 2)), joined(right_terms(lead_in[...], 2))
            )
            forward(0).start()

        @pl.when(k >= 3)
        def _():
            pass_on(k - 2)

    def trailing(s):
        def columns(j, carry):
            cols = pl.ds(pl.multiple_of(j * WIDE, WIDE), WIDE)
            right = cat_right[cols, :]

            def lower(i, carry):
                at = pl.ds(pl.multiple_of(i * WIDE, WIDE), WIDE)
                a_mat[at, cols] = a_mat[at, cols] - dot_nt(cat_left[at, :], right)
                return carry

            lax.fori_loop(j, SUPER, lower, 0)
            r_mat[:, cols] = r_mat[:, cols] - dot_nt(cat_rows[...], right[:, : 3 * WIDE])
            return carry

        lax.fori_loop(s + 1, SUPER, columns, 0)

    def super_step(s, carry):
        half_step(s, 0)
        half_step(s, 1)

        @pl.when(s == 0)
        def _():
            for copy in late + late_pairs:
                copy.wait()

        trailing(s)
        return carry

    lax.fori_loop(0, SUPER, super_step, 0)

    def stage_copy(stage, d):
        slot = acc_corner.at[stage, spots[stage]]
        return remote(slot, slot, sum_send.at[stage, d - 1], sum_recv.at[stage, d - 1], partner(stage, d))

    def stage_start(stage):
        for d in (1, 2, 3):
            stage_copy(stage, d).start()

    def stage_end(stage):
        for d in (1, 2, 3):
            stage_copy(stage, d).wait()
        return acc_corner[stage, 0] + acc_corner[stage, 1] + acc_corner[stage, 2] + acc_corner[stage, 3]

    def next_stage(stage):
        total = stage_end(stage)
        acc_corner[stage + 1, spots[stage + 1]] = total
        stage_start(stage + 1)

    to_sibling(STEPS - 2).wait()
    to_sibling(STEPS - 1).wait()
    for task in local_tasks(SUPER - 1):
        task()
    stage_start(0)
    second_hop(STEPS - 2)
    third_hop(STEPS - 3)
    pass_on(STEPS - 3)
    second_hop(STEPS - 1)
    third_hop(STEPS - 2)
    await_received(STEPS - 4)
    await_received(STEPS - 3)
    for task in received_tasks(SUPER - 2):
        task()
    third_hop(STEPS - 1)
    pass_on(STEPS - 2)
    await_received(STEPS - 2)
    for task in received_block_tasks(STEPS - 2):
        task()
    next_stage(0)
    pass_on(STEPS - 1)
    next_stage(1)
    await_received(STEPS - 1)
    for task in received_block_tasks(STEPS - 1):
        task()
    fixed_sum[...] = fixed_sum[...] - stage_end(2)
    for k in range(STEPS - IN_FLIGHT, STEPS):
        sent(k)


def store(
    solved, factor, acc_diag, acc_lower, acc_upper, acc_fixed, fixed_sum,
    o_pivot, o_left, o_right, o_arrow, o_diag, o_lower, o_upper, o_fixed, o_corner, sem,
):
    copies = [
        (acc_diag, o_diag), (acc_lower, o_lower), (acc_upper, o_upper), (acc_fixed, o_fixed), (fixed_sum, o_corner),
    ]
    for k in range(STEPS):
        cols = pl.ds(k * BLOCK, BLOCK)
        copies += [
            (factor.at[k], o_pivot.at[0, :, cols]),
            (solved.at[k, LOW:, :], o_left.at[0, :, cols]),
            (solved.at[k, 0:HALF, :], o_right.at[0, :, cols]),
            (solved.at[k, HALF:LOW, :], o_arrow.at[0, :, cols]),
        ]
    copies = [pltpu.make_async_copy(a, b, sem.at[n]) for n, (a, b) in enumerate(copies)]
    for copy in copies:
        copy.start()
    for copy in copies:
        copy.wait()


def local(count, diag_block, coupling, arrow, corner):
    def shape(*dims):
        return jax.ShapeDtypeStruct(dims, F32)

    block = shape(1, HALF, NODES)
    strip = shape(1, FX, NODES)
    fixed = shape(FX, 64)
    any_space = pl.BlockSpec(memory_space=pl.ANY)
    hbm_space = pl.BlockSpec(memory_space=pltpu.HBM)
    vmem_space = pl.BlockSpec(memory_space=pltpu.VMEM)
    dma = pltpu.SemaphoreType.DMA
    held = pl.pallas_call(
        functools.partial(eliminate, count),
        out_shape=(shape(STEPS, ROWS, BLOCK), shape(STEPS, HALF, BLOCK), block, block, block, strip, fixed),
        in_specs=[hbm_space] * 4,
        out_specs=[vmem_space] * 7,
        scratch_shapes=[
            pltpu.VMEM((NODES, NODES), F32),
            pltpu.VMEM((ROWS, NODES), F32),
            pltpu.VMEM((NODES, HALF), F32),
            pltpu.VMEM((STEPS, ROWS, BLOCK), F32),
            pltpu.VMEM((STEPS, LOW, BLOCK), F32),
            pltpu.VMEM((STEPS, HALF, BLOCK), F32),
            pltpu.VMEM((STEPS, RELAY, BLOCK), F32),
            pltpu.VMEM((STEPS, RELAY, BLOCK), F32),
            pltpu.VMEM((3, 4, FX, 64), F32),
            pltpu.VMEM((NODES, 6 * WIDE), BF16),
            pltpu.VMEM((NODES, 6 * WIDE), BF16),
            pltpu.VMEM((ROWS, 3 * WIDE), BF16),
            pltpu.VMEM((BLOCK, 2 * BLOCK), F32),
            pltpu.VMEM((BLOCK, 2 * BLOCK), F32),
            pltpu.VMEM((BLOCK, BLOCK), F32),
            pltpu.VMEM((BLOCK, BLOCK), F32),
            dma((SUPER,)), dma((SUPER,)), dma((2,)), dma((4,)),
            dma((SUPER,)), dma((SUPER,)), dma((2,)), dma((2,)),
            dma((STEPS,)), dma((STEPS,)), dma((STEPS,)), dma((STEPS,)),
            dma((STEPS,)), dma((STEPS,)), dma((STEPS,)), dma((STEPS,)),
            dma((3, STEPS)), dma((3, STEPS)), dma((3, 3)), dma((3, 3)), dma, dma,
        ],
        compiler_params=pltpu.CompilerParams(
            collective_id=0, has_side_effects=True, vmem_limit_bytes=40 * 2**20
        ),
        cost_estimate=pl.CostEstimate(flops=30_000_000_000, bytes_accessed=22_000_000, transcendentals=0),
        name="eliminate",
    )(*[pltpu.with_memory_space_constraint(x, pltpu.HBM) for x in (diag_block, coupling, arrow, corner)])
    return pl.pallas_call(
        store,
        out_shape=(block, block, block, strip, block, block, block, strip, fixed),
        in_specs=[vmem_space] * 7,
        out_specs=[any_space] * 9,
        scratch_shapes=[dma((5 + 4 * STEPS,))],
        compiler_params=pltpu.CompilerParams(vmem_limit_bytes=16 * 2**20),
        name="store",
    )(*held)


def solution(mesh):
    rows = P("tm", "blk", None)
    placed = (rows, rows, rows, P("blk", None))
    return jax.shard_map(
        functools.partial(local, mesh.shape["tm"]),
        mesh=mesh,
        in_specs=placed,
        out_specs=(rows,) * 8 + (P("blk", None),),
        check_vma=False,
    )
```

```python
import functools

import jax
import jax.numpy as jnp
from jax import lax
from jax.experimental import pallas as pl
from jax.experimental.pallas import tpu as pltpu
from jax.sharding import PartitionSpec as P

MESH = pl.DeviceIdType.MESH
F32 = jnp.float32
BF16 = jnp.bfloat16
NODES = 1024
HALF = 512
FX = 32
BLOCK = 128
STEPS = NODES // BLOCK
ROWS = 2 * HALF + FX
MICRO = 32
IN_FLIGHT = 2
WIDE = 2 * BLOCK
SUPER = NODES // WIDE
LOW = HALF + FX
CUT = ROWS - 240
RELAY = ROWS - CUT


def dot_nt(left, right):
    return lax.dot_general(left, right, (((1,), (1,)), ((), ())), preferred_element_type=F32)


def split(value, parts):
    out = []
    for _ in range(parts):
        piece = value.astype(BF16)
        out.append(piece)
        value = value - piece.astype(F32)
    return out


def left_terms(value, parts=3):
    if parts == 2:
        a, b = split(value, 2)
        return [a, a, b]
    a, b, c = split(value, 3)
    return [a, a, b, a, b, c]


def right_terms(value, parts=3):
    if parts == 2:
        a, b = split(value, 2)
        return [a, b, a]
    a, b, c = split(value, 3)
    return [a, b, a, c, b, a]


def joined(terms):
    return jnp.concatenate(terms, axis=1)


def left_pair(first, second):
    return joined(left_terms(joined([first, second]), 2))


def right_pair(first, second):
    return joined(right_terms(joined([first, second]), 2))


def factor_inverse(work, done, tasks=(), every=16):
    groups = MICRO // 8
    tasks = list(tasks)
    row_id = lax.broadcasted_iota(jnp.int32, (8, 2 * BLOCK), 0)
    twice = lambda value: jnp.concatenate([value, value], axis=1)
    for base in range(0, BLOCK, MICRO):
        rows = [work[base + 8 * g : base + 8 * g + 8, :] for g in range(groups)]
        cols = [
            [jnp.broadcast_to(rows[g][:, base + m : base + m + 1], (8, BLOCK)) for m in range(8 * g + 8)]
            for g in range(groups)
        ]
        final = [jnp.zeros((8, 2 * BLOCK), F32) for _ in range(groups)]
        for j in range(MICRO):
            if tasks and (base + j) % every == every - 1:
                tasks.pop(0)()
            gj, rj = divmod(j, 8)
            inverse = lax.rsqrt(jnp.broadcast_to(cols[gj][j][rj : rj + 1, :], (8, BLOCK)))
            pivot_row = jnp.broadcast_to(rows[gj][rj : rj + 1, :], (8, 2 * BLOCK)) * twice(inverse)
            final[gj] = jnp.where(row_id == rj, pivot_row, final[gj])
            low = [None] * groups
            for g in range(gj, groups):
                low[g] = cols[g][j] * inverse
                rows[g] = rows[g] - twice(low[g]) * pivot_row
            for m in range(j + 1, MICRO):
                gm, rm = divmod(m, 8)
                factor = jnp.broadcast_to(low[gm][rm : rm + 1, :], (8, BLOCK))
                for g in range(gm, groups):
                    cols[g][m] = cols[g][m] - low[g] * factor
        panel = jnp.concatenate(final, axis=0)
        done[base : base + MICRO, :] = panel
        rest = base + MICRO
        if rest < BLOCK:
            update = lax.dot_general(
                panel[:, :BLOCK],
                panel,
                (((0,), (0,)), ((), ())),
                precision=lax.Precision.HIGHEST,
                preferred_element_type=F32,
            )
            work[rest:, :] = work[rest:, :] - update[rest:, :]
    for task in tasks:
        task()


def eliminate(
    count,
    diag, coupling, arrow, corner,
    solved, factor, acc_diag, acc_lower, acc_upper, acc_fixed, fixed_sum,
    a_mat, r_mat, turn, arrived, sibling, forwarded, relay_a, relay_b,
    acc_corner, cat_left, cat_right, cat_rows, work, done, lead, lead_in,
    a_sem, r_sem, turn_sem, load_sem, a_send, a_recv, turn_send, turn_recv,
    top_send, top_recv, low_send, low_recv, sib_send, sib_recv, fwd_send, fwd_recv,
    hop_send, hop_recv, sum_send, sum_recv, lead_send, lead_recv,
):
    p = lax.axis_index("tm")
    c = lax.axis_index("blk")
    other = 1 - c
    strides = (16, 4, 1)
    spots = [lax.rem(p // s, 4) for s in strides]
    spot = spots[2]
    row_start = p - spot

    def partner(stage, d):
        return (p + (lax.rem(spots[stage] + d, 4) - spots[stage]) * strides[stage], c)

    def in_row(d):
        return row_start + lax.rem(spot + d, 4)

    nxt = (lax.rem(p + 1, count), c)
    prv_tm = lax.rem(p + count - 1, count)
    prv = (prv_tm, c)
    sib = (p, other)
    minus = (in_row(3), c)
    plus = (in_row(1), c)
    hop_to = (jnp.where(spot == 2, lax.rem(row_start + 5, count), minus[0]), c)
    hop_from = (jnp.where(spot == 1, lax.rem(row_start + count - 2, count), plus[0]), c)

    own_rows = pl.ds(pl.multiple_of(c * HALF, HALF), HALF)
    other_cols = pl.ds(pl.multiple_of(other * HALF, HALF), HALF)

    def remote(src, dst, send, recv, device):
        return pltpu.make_async_remote_copy(
            src_ref=src, dst_ref=dst, send_sem=send, recv_sem=recv, device_id=device, device_id_type=MESH
        )

    barrier = pltpu.get_barrier_semaphore()
    senders = [prv, sib, plus, hop_from] + [partner(s, d) for s in range(3) for d in (1, 2, 3)]
    for device in senders:
        pl.semaphore_signal(barrier, inc=1, device_id=device, device_id_type=MESH)

    def wide(s):
        return pl.ds(s * WIDE, WIDE)

    def half_rows(q):
        return pl.ds(pl.multiple_of(c * HALF + q * WIDE, WIDE), WIDE)

    a_loads = [
        pltpu.make_async_copy(diag.at[1, :, wide(s)], a_mat.at[own_rows, wide(s)], a_sem.at[s]) for s in range(SUPER)
    ]
    r_loads = [
        pltpu.make_async_copy(coupling.at[1, :, wide(s)], r_mat.at[0:HALF, wide(s)], r_sem.at[s])
        for s in range(SUPER)
    ]
    turn_loads = [
        pltpu.make_async_copy(coupling.at[0, wide(q), own_rows], turn.at[half_rows(q), :], turn_sem.at[q])
        for q in range(2)
    ]
    loads = [
        pltpu.make_async_copy(arrow.at[1], r_mat.at[HALF:LOW, :], load_sem.at[0]),
        pltpu.make_async_copy(diag.at[0], acc_diag.at[0], load_sem.at[1]),
        pltpu.make_async_copy(arrow.at[0], acc_fixed.at[0], load_sem.at[2]),
        pltpu.make_async_copy(corner, fixed_sum, load_sem.at[3]),
    ]
    a_pairs = [
        remote(diag.at[1, :, wide(s)], a_mat.at[own_rows, wide(s)], a_send.at[s], a_recv.at[s], sib)
        for s in range(SUPER)
    ]
    turn_pairs = [
        remote(coupling.at[0, wide(q), other_cols], turn.at[half_rows(q), :], turn_send.at[q], turn_recv.at[q], sib)
        for q in range(2)
    ]
    early = [a_loads[0], turn_loads[0], r_loads[0], loads[0]]
    late = [a_loads[1], r_loads[1], turn_loads[1], a_loads[2], r_loads[2], a_loads[3], r_loads[3]] + loads[1:]
    early_pairs = [a_pairs[0], turn_pairs[0]]
    late_pairs = [a_pairs[1], turn_pairs[1], a_pairs[2], a_pairs[3]]
    for copy in early:
        copy.start()
    pl.semaphore_wait(barrier, len(senders))
    for copy in early_pairs:
        copy.start()
    raw_top = remote(
        coupling.at[1, :, pl.ds(0, BLOCK)], arrived.at[0, 0:HALF, :], top_send.at[0], top_recv.at[0], nxt
    )
    raw_top.start()
    lead_copy = remote(lead, lead_in, lead_send, lead_recv, nxt)
    for copy in late + late_pairs:
        copy.start()
    r_mat[LOW:, :] = jnp.zeros((HALF, NODES), F32)
    acc_lower[...] = jnp.zeros_like(acc_lower)
    acc_upper[...] = jnp.zeros_like(acc_upper)
    acc_corner[0, spots[0]] = jnp.zeros((FX, 64), F32)
    identity = (
        lax.broadcasted_iota(jnp.int32, (BLOCK, BLOCK), 0) == lax.broadcasted_iota(jnp.int32, (BLOCK, BLOCK), 1)
    ).astype(F32)
    open_end = jnp.where(p < count - 1, 1.0, 0.0).astype(F32)
    open_start = jnp.where(p > 0, 1.0, 0.0).astype(F32)
    for copy in early + early_pairs:
        copy.wait()

    def top_copy(k):
        return remote(solved.at[k, 0:HALF, :], arrived.at[k, 0:HALF, :], top_send.at[k], top_recv.at[k], nxt)

    def low_copy(k):
        return remote(solved.at[k, HALF:CUT, :], arrived.at[k, HALF:CUT, :], low_send.at[k], low_recv.at[k], nxt)

    def hop(stage, k):
        if stage == 0:
            return remote(solved.at[k, CUT:, :], relay_a.at[k], hop_send.at[0, k], hop_recv.at[0, k], minus)
        if stage == 1:
            return remote(relay_a.at[k], relay_b.at[k], hop_send.at[1, k], hop_recv.at[1, k], hop_to)
        return remote(relay_b.at[k], arrived.at[k, CUT:, :], hop_send.at[2, k], hop_recv.at[2, k], minus)

    def to_sibling(k):
        return remote(solved.at[k, HALF:, :], sibling.at[k], sib_send.at[k], sib_recv.at[k], sib)

    def forward(k):
        return remote(arrived.at[k, 0:HALF, :], forwarded.at[k], fwd_send.at[k], fwd_recv.at[k], sib)

    def tile(base, q):
        return pl.ds(pl.multiple_of(base * HALF + q * WIDE, WIDE), WIDE)

    def product_tasks(top, low, mine, theirs, first, second):
        tasks = []
        for right, base in ((mine, c), (theirs, other)):
            for q in range(2):
                piece = right[q * WIDE : (q + 1) * WIDE, :]
                cols = tile(base, q)

                def upper(piece=piece, cols=cols):
                    first[0, :, cols] = first[0, :, cols] - dot_nt(top, piece)

                def lower(piece=piece, cols=cols):
                    value = dot_nt(low, piece)
                    acc_fixed[0, :, cols] = acc_fixed[0, :, cols] - value[0:FX, :]
                    second[0, :, cols] = second[0, :, cols] - value[FX:, :]

                tasks += [upper, lower]
        return tasks

    def local_tasks(s):
        e, o = 2 * s, 2 * s + 1
        low = cat_rows[HALF:, :]
        far = right_pair(sibling[e], sibling[o])
        near = joined([low[:, 0:WIDE], low[:, 2 * WIDE :], low[:, 0:WIDE]])

        def fixed():
            mid = low[0:FX, :]
            own, their = dot_nt(mid, near[0:FX, :]), dot_nt(mid, far[0:FX, :])
            both = jnp.where(c == 0, joined([own, their]), joined([their, own]))
            acc_corner[0, spots[0]] = acc_corner[0, spots[0]] + both

        return product_tasks(cat_rows[0:HALF, :], low, near[FX:, :], far[FX:, :], acc_upper, acc_diag) + [fixed]

    def received_tasks(s):
        e, o = 2 * s, 2 * s + 1
        return product_tasks(
            left_pair(arrived[e, 0:HALF, :], arrived[o, 0:HALF, :]),
            left_pair(arrived[e, HALF:, :], arrived[o, HALF:, :]),
            right_pair(arrived[e, 0:HALF, :], arrived[o, 0:HALF, :]),
            right_pair(forwarded[e], forwarded[o]),
            acc_diag,
            acc_lower,
        )

    def received_block_tasks(k):
        return product_tasks(
            joined(left_terms(arrived[k, 0:HALF, :], 2)),
            joined(left_terms(arrived[k, HALF:, :], 2)),
            joined(right_terms(arrived[k, 0:HALF, :], 2)),
            joined(right_terms(forwarded[k], 2)),
            acc_diag,
            acc_lower,
        )

    def last_block(k):
        sides = (
            (joined(right_terms(arrived[k, 0:HALF, :], 2)), c),
            (joined(right_terms(forwarded[k], 2)), other),
        )
        top = joined(left_terms(arrived[k, 0:HALF, :], 2))
        for right, base in sides:
            for q in range(2):
                cols = tile(base, q)
                piece = right[q * WIDE : (q + 1) * WIDE, :]
                acc_diag[0, :, cols] = acc_diag[0, :, cols] - dot_nt(top, piece)
        low_copy(k).wait_recv()
        hop(2, k).wait()
        low = joined(left_terms(arrived[k, HALF:, :], 2))
        for right, base in sides:
            for q in range(2):
                cols = tile(base, q)
                value = dot_nt(low, right[q * WIDE : (q + 1) * WIDE, :])
                acc_fixed[0, :, cols] = acc_fixed[0, :, cols] - value[0:FX, :]
                acc_lower[0, :, cols] = acc_lower[0, :, cols] - value[FX:, :]

    def await_received(k):
        forward(k).wait()
        low_copy(k).wait_recv()
        hop(2, k).wait()

    def half_step(s, h):
        k = 2 * s + h
        cols = pl.ds(pl.multiple_of(k * BLOCK, BLOCK), BLOCK)
        after = pl.ds(pl.multiple_of((2 * s + 1) * BLOCK, BLOCK), BLOCK)
        work[:, :BLOCK] = a_mat[cols, cols]
        work[:, BLOCK:] = identity
        if h == 0:

            @pl.when(s == 0)
            def _():
                factor_inverse(work, done)

            @pl.when(s >= 1)
            def _():
                to_sibling(2 * s - 2).wait()
                to_sibling(2 * s - 1).wait()
                factor_inverse(work, done, local_tasks(s - 1))
        else:

            @pl.when(s < 2)
            def _():
                factor_inverse(work, done)

            @pl.when(s >= 2)
            def _():
                await_received(2 * s - 4)
                await_received(2 * s - 3)
                factor_inverse(work, done, received_tasks(s - 2))

        inverse = joined(right_terms(done[:, BLOCK:]))
        if h == 0:
            beside = joined(right_terms(dot_nt(joined(left_terms(a_mat[after, cols])), inverse)))

        r_mat[0:HALF, cols] = r_mat[0:HALF, cols] * open_end
        r_mat[LOW:, cols] = r_mat[LOW:, cols] + turn[cols, :].T
        value = dot_nt(joined(left_terms(r_mat[:, cols], 2)), inverse[:, : 3 * BLOCK])
        solved[k] = value
        @pl.when(k >= IN_FLIGHT)
        def _():
            sent(k - IN_FLIGHT)

        if h == 0:

            @pl.when(s == 0)
            def _():
                lead[...] = done[:, BLOCK:]
                lead_copy.start()

            @pl.when(s > 0)
            def _():
                top_copy(k).start()
        else:
            top_copy(k).start()
        to_sibling(k).start()

        low_copy(k).start()
        hop(0, k).start()

        terms = left_terms(value, 2)
        for t in range(3):
            cat_rows[:, t * WIDE + h * BLOCK : t * WIDE + (h + 1) * BLOCK] = terms[t]
        if h == 0:
            r_mat[:, after] = r_mat[:, after] - dot_nt(joined(terms), beside[:, : 3 * BLOCK])

        def factor_rows(i, carry):
            at = pl.ds(pl.multiple_of(i * WIDE, WIDE), WIDE)
            value = dot_nt(joined(left_terms(a_mat[at, cols])), inverse)
            row = lax.broadcasted_iota(jnp.int32, (WIDE, BLOCK), 0) + i * WIDE
            col = lax.broadcasted_iota(jnp.int32, (WIDE, BLOCK), 1) + k * BLOCK
            value = jnp.where(row >= col, value, 0.0)

            @pl.when(i // 2 == c)
            def _():
                factor[k, pl.ds(pl.multiple_of((i - 2 * c) * WIDE, WIDE), WIDE), :] = value

            a, b, d = split(value, 3)
            for t, (x, y) in enumerate(zip([a, a, b, a, b, d], [a, b, a, d, b, a])):
                cat_left[at, t * WIDE + h * BLOCK : t * WIDE + (h + 1) * BLOCK] = x
                cat_right[at, t * WIDE + h * BLOCK : t * WIDE + (h + 1) * BLOCK] = y
            if h == 0:
                a_mat[at, after] = a_mat[at, after] - dot_nt(joined([a, a, b, a, b, d]), beside)
            return carry

        lax.fori_loop(s, SUPER, factor_rows, 0)

        def clear_rows(i, carry):
            @pl.when(i // 2 == c)
            def _():
                factor[k, pl.ds(pl.multiple_of((i - 2 * c) * WIDE, WIDE), WIDE), :] = jnp.zeros((WIDE, BLOCK), F32)

            return carry

        lax.fori_loop(0, s, clear_rows, 0)
        if h == 0:
            service(k)
        else:

            @pl.when(s < SUPER - 1)
            def _():
                service(k)


    def sent(k):
        top_copy(k).wait_send()
        low_copy(k).wait_send()

    def pass_on(k):
        top_copy(k).wait_recv()
        forward(k).start()

    def second_hop(k):
        hop(0, k).wait()
        hop(1, k).start()

    def third_hop(k):
        hop(1, k).wait()
        hop(2, k).start()

    def service(k):
        @pl.when(k >= 1)
        def _():
            second_hop(k - 1)

        @pl.when(k >= 2)
        def _():
            third_hop(k - 2)

        @pl.when(k == 2)
        def _():
            raw_top.wait_recv()
            lead_copy.wait()
            raw = arrived[0, 0:HALF, :] * open_start
            arrived[0, 0:HALF, :] = dot_nt(
                joined(left_terms(raw, 2)), joined(right_terms(lead_in[...], 2))
            )
            forward(0).start()

        @pl.when(k >= 3)
        def _():
            pass_on(k - 2)

    def trailing(s):
        def columns(j, carry):
            cols = pl.ds(pl.multiple_of(j * WIDE, WIDE), WIDE)
            right = cat_right[cols, :]

            def lower(i, carry):
                at = pl.ds(pl.multiple_of(i * WIDE, WIDE), WIDE)
                a_mat[at, cols] = a_mat[at, cols] - dot_nt(cat_left[at, :], right)
                return carry

            lax.fori_loop(j, SUPER, lower, 0)
            r_mat[:, cols] = r_mat[:, cols] - dot_nt(cat_rows[...], right[:, : 3 * WIDE])
            return carry

        lax.fori_loop(s + 1, SUPER, columns, 0)

    def super_step(s, carry):
        half_step(s, 0)
        half_step(s, 1)

        @pl.when(s == 0)
        def _():
            for copy in late + late_pairs:
                copy.wait()

        trailing(s)
        return carry

    lax.fori_loop(0, SUPER, super_step, 0)

    def stage_copy(stage, d):
        slot = acc_corner.at[stage, spots[stage]]
        return remote(slot, slot, sum_send.at[stage, d - 1], sum_recv.at[stage, d - 1], partner(stage, d))

    def stage_start(stage):
        for d in (1, 2, 3):
            stage_copy(stage, d).start()

    def stage_end(stage):
        for d in (1, 2, 3):
            stage_copy(stage, d).wait()
        return acc_corner[stage, 0] + acc_corner[stage, 1] + acc_corner[stage, 2] + acc_corner[stage, 3]

    def next_stage(stage):
        total = stage_end(stage)
        acc_corner[stage + 1, spots[stage + 1]] = total
        stage_start(stage + 1)

    to_sibling(STEPS - 2).wait()
    to_sibling(STEPS - 1).wait()
    for task in local_tasks(SUPER - 1):
        task()
    stage_start(0)
    second_hop(STEPS - 2)
    third_hop(STEPS - 3)
    pass_on(STEPS - 3)
    second_hop(STEPS - 1)
    third_hop(STEPS - 2)
    await_received(STEPS - 4)
    await_received(STEPS - 3)
    for task in received_tasks(SUPER - 2):
        task()
    third_hop(STEPS - 1)
    pass_on(STEPS - 2)
    await_received(STEPS - 2)
    for task in received_block_tasks(STEPS - 2):
        task()
    next_stage(0)
    pass_on(STEPS - 1)
    next_stage(1)
    forward(STEPS - 1).wait()
    last_block(STEPS - 1)
    fixed_sum[...] = fixed_sum[...] - stage_end(2)
    for k in range(STEPS - IN_FLIGHT, STEPS):
        sent(k)


def store(
    solved, factor, acc_diag, acc_lower, acc_upper, acc_fixed, fixed_sum,
    o_pivot, o_left, o_right, o_arrow, o_diag, o_lower, o_upper, o_fixed, o_corner, sem,
):
    copies = [
        (acc_diag, o_diag), (acc_lower, o_lower), (acc_upper, o_upper), (acc_fixed, o_fixed), (fixed_sum, o_corner),
    ]
    for k in range(STEPS):
        cols = pl.ds(k * BLOCK, BLOCK)
        copies += [
            (factor.at[k], o_pivot.at[0, :, cols]),
            (solved.at[k, LOW:, :], o_left.at[0, :, cols]),
            (solved.at[k, 0:HALF, :], o_right.at[0, :, cols]),
            (solved.at[k, HALF:LOW, :], o_arrow.at[0, :, cols]),
        ]
    copies = [pltpu.make_async_copy(a, b, sem.at[n]) for n, (a, b) in enumerate(copies)]
    for copy in copies:
        copy.start()
    for copy in copies:
        copy.wait()


def local(count, diag_block, coupling, arrow, corner):
    def shape(*dims):
        return jax.ShapeDtypeStruct(dims, F32)

    block = shape(1, HALF, NODES)
    strip = shape(1, FX, NODES)
    fixed = shape(FX, 64)
    any_space = pl.BlockSpec(memory_space=pl.ANY)
    hbm_space = pl.BlockSpec(memory_space=pltpu.HBM)
    vmem_space = pl.BlockSpec(memory_space=pltpu.VMEM)
    dma = pltpu.SemaphoreType.DMA
    held = pl.pallas_call(
        functools.partial(eliminate, count),
        out_shape=(shape(STEPS, ROWS, BLOCK), shape(STEPS, HALF, BLOCK), block, block, block, strip, fixed),
        in_specs=[hbm_space] * 4,
        out_specs=[vmem_space] * 7,
        scratch_shapes=[
            pltpu.VMEM((NODES, NODES), F32),
            pltpu.VMEM((ROWS, NODES), F32),
            pltpu.VMEM((NODES, HALF), F32),
            pltpu.VMEM((STEPS, ROWS, BLOCK), F32),
            pltpu.VMEM((STEPS, LOW, BLOCK), F32),
            pltpu.VMEM((STEPS, HALF, BLOCK), F32),
            pltpu.VMEM((STEPS, RELAY, BLOCK), F32),
            pltpu.VMEM((STEPS, RELAY, BLOCK), F32),
            pltpu.VMEM((3, 4, FX, 64), F32),
            pltpu.VMEM((NODES, 6 * WIDE), BF16),
            pltpu.VMEM((NODES, 6 * WIDE), BF16),
            pltpu.VMEM((ROWS, 3 * WIDE), BF16),
            pltpu.VMEM((BLOCK, 2 * BLOCK), F32),
            pltpu.VMEM((BLOCK, 2 * BLOCK), F32),
            pltpu.VMEM((BLOCK, BLOCK), F32),
            pltpu.VMEM((BLOCK, BLOCK), F32),
            dma((SUPER,)), dma((SUPER,)), dma((2,)), dma((4,)),
            dma((SUPER,)), dma((SUPER,)), dma((2,)), dma((2,)),
            dma((STEPS,)), dma((STEPS,)), dma((STEPS,)), dma((STEPS,)),
            dma((STEPS,)), dma((STEPS,)), dma((STEPS,)), dma((STEPS,)),
            dma((3, STEPS)), dma((3, STEPS)), dma((3, 3)), dma((3, 3)), dma, dma,
        ],
        compiler_params=pltpu.CompilerParams(
            collective_id=0, has_side_effects=True, vmem_limit_bytes=40 * 2**20
        ),
        cost_estimate=pl.CostEstimate(flops=30_000_000_000, bytes_accessed=22_000_000, transcendentals=0),
        name="eliminate",
    )(*[pltpu.with_memory_space_constraint(x, pltpu.HBM) for x in (diag_block, coupling, arrow, corner)])
    return pl.pallas_call(
        store,
        out_shape=(block, block, block, strip, block, block, block, strip, fixed),
        in_specs=[vmem_space] * 7,
        out_specs=[any_space] * 9,
        scratch_shapes=[dma((5 + 4 * STEPS,))],
        compiler_params=pltpu.CompilerParams(vmem_limit_bytes=16 * 2**20),
        name="store",
    )(*held)


def solution(mesh):
    rows = P("tm", "blk", None)
    placed = (rows, rows, rows, P("blk", None))
    return jax.shard_map(
        functools.partial(local, mesh.shape["tm"]),
        mesh=mesh,
        in_specs=placed,
        out_specs=(rows,) * 8 + (P("blk", None),),
        check_vma=False,
    )
```
